256 devices in a mesh: row: 16 (over z, core), col: 16 (over y, x).
Axes of the slice: x: 4, y: 4, z: 8, core: 2. Of those that a mesh axis runs over, the one named last changes fastest.
Arguments:
- a_matrix: bfloat16 [32768, 24576], P('row', 'col'), may hold values from -6 to 6
- omega: bfloat16 [24576, 512], P('col'), may hold values from -0.0390625 to 0.0390625
- leaf_pivots: int32 [16, 2048], P('row'), may hold values from 0 to 2047, each once within a row
- upper_pivots: int32 [3, 8, 1024], replicated, may hold values from 0 to 1023, each once within a row
- ranks: int32 [4, 16], replicated, may hold values from 256 to 512
Outputs:
- leaf_interp: float32 [16, 1536, 512], P('row', 'col')
- upper_interp: float32 [3, 16, 512, 512], P(None, 'row', 'col')
The draws below stay inside these ranges and needn't reach their ends.
Inputs may be any that keep to these rules, and one draw needn't show every extreme that they name: Each row of leaf_pivots and of upper_pivots is a permutation. Rows of ranks beyond the level's node count are not read.
All inputs are finite; a program needn't handle non-finite values. Where the reference program divides by a largest or mean magnitude, that divisor is 1e-20 or more.
Results may differ from the reference program's by a relative error of at most 0.0003.
Values sent between devices are 32-bit elements; how exact they have to be, the bound alone decides.
No kernel may reach another device: no remote copies, remote signals or barrier semaphores. Data moves between devices by JAX's collectives and lax.ppermute only.
A program may use at most 128 MiB of HBM per device.

```python
import math
import jax
import jax.numpy as jnp
from jax import lax

LEAF = 2048
K = 512
S = 512
LEVELS = 4
NEWTON = 6
NC = 24576
ROWS = 32768
N_ROW = 16


def touch_ends(array, rng, least, top_value):
    index_at = [jax.random.randint(jax.random.fold_in(rng, axis), (), 0, length) for axis, length in enumerate(array.shape)]
    main_axis = array.shape.index(max(array.shape))
    next_to = index_at[:main_axis] + [(index_at[main_axis] + 1) % array.shape[main_axis]] + index_at[main_axis + 1:]
    return array.at[tuple(index_at)].set(least).at[tuple(next_to)].set(top_value)


def steps_of(key, extent, shards, least, largest):
    level = 1.0
    for axis_at, shards_of in shards:
        steps = jax.random.uniform(jax.random.fold_in(jax.random.fold_in(key, 6), axis_at), (shards_of,), jnp.float32, least / len(shards), largest / len(shards))
        level = level * jnp.repeat(jnp.exp(steps), extent[axis_at] // shards_of).reshape((-1,) + (1,) * (len(extent) - 1 - axis_at))
    return level


def noise(rng, extent, spread, most, split=(), kind=jnp.bfloat16):
    values = spread * jax.random.normal(rng, extent, jnp.float32)
    if split:
        values = values * steps_of(rng, extent, split, -0.22, 0.18)
    return jnp.clip(values, -most, most).astype(kind)


def setup_inputs(seed: int = 0) -> dict:
    arg_keys = jax.random.split(jax.random.key(seed), 6)
    a_matrix = noise(arg_keys[0], (ROWS, NC), 1.0, 6.0, ((0, 16), (1, 16)))
    omega = noise(arg_keys[1], (NC, S), NC ** -0.5, 0.0390625, ((0, 16),))
    leaf_pivots = jax.vmap(lambda own: jax.random.permutation(own, LEAF))(jax.random.split(arg_keys[2], N_ROW)).reshape((N_ROW, LEAF)).astype(jnp.int32)
    upper_pivots = jax.vmap(lambda own: jax.random.permutation(own, 2 * K))(jax.random.split(arg_keys[3], (LEVELS - 1) * (N_ROW // 2))).reshape((LEVELS - 1, N_ROW // 2, 2 * K)).astype(jnp.int32)
    ranks = touch_ends(jax.random.randint(arg_keys[4], (LEVELS, N_ROW), K // 2, K + 1), jax.random.fold_in(arg_keys[4], 1), K // 2, K).astype(jnp.int32)
    return dict(a_matrix=a_matrix, omega=omega, leaf_pivots=leaf_pivots, upper_pivots=upper_pivots, ranks=ranks)


def compress(node_rows, pivots, node_rank):
    permuted = jnp.take(node_rows, pivots.astype(jnp.int32), axis=0)
    kept_mask = (jnp.arange(K) < node_rank).astype(jnp.float32)
    return (permuted[:K] * kept_mask[:, None], permuted[K:])

def approximate_inverse(gram_matrix):
    identity = jnp.eye(K, dtype=jnp.float32)
    bound = jnp.max(lax.optimization_barrier(jnp.sum(jnp.abs(gram_matrix), axis=1)))
    inverse = 2.0 / bound * identity - gram_matrix / (bound * bound)
    for step in range(NEWTON - 1):
        product = jnp.dot(gram_matrix, inverse, precision=lax.Precision.HIGHEST, preferred_element_type=jnp.float32)
        inverse = jnp.dot(inverse, 2.0 * identity - product, precision=lax.Precision.HIGHEST, preferred_element_type=jnp.float32)
    return inverse

def interpolate(skeleton, redundant):
    gram_sum = jnp.dot(skeleton, skeleton.T, precision=lax.Precision.HIGHEST, preferred_element_type=jnp.float32)
    cross_sum = jnp.dot(redundant, skeleton.T, precision=lax.Precision.HIGHEST, preferred_element_type=jnp.float32)
    gram_matrix = gram_sum / (8.0 * S) + jnp.eye(K, dtype=jnp.float32)
    inverse = approximate_inverse(gram_matrix)
    return jnp.dot(cross_sum / math.sqrt(S), inverse, precision=lax.Precision.HIGHEST, preferred_element_type=jnp.float32)

def reference(a_matrix, omega, leaf_pivots, upper_pivots, ranks):
    samples = jnp.dot(a_matrix, omega, preferred_element_type=jnp.float32).reshape(N_ROW, LEAF, S)
    skeleton, redundant = jax.vmap(compress)(samples, leaf_pivots, ranks[0])
    leaf_interp = jax.vmap(interpolate)(skeleton, redundant)
    upper_list = []
    for level_index in range(1, LEVELS):
        node_count = N_ROW >> level_index
        node_rows = skeleton.reshape(node_count, 2 * K, S)
        skeleton, redundant = jax.vmap(compress)(node_rows, upper_pivots[level_index - 1, :node_count], ranks[level_index, :node_count])
        node_interp = jax.vmap(interpolate)(skeleton, redundant)
        upper_list.append(jnp.repeat(node_interp, 2 ** level_index, axis=0))
    return (leaf_interp, jnp.stack(upper_list))
```

```python
import math

import jax
import jax.numpy as jnp
from jax import lax
from jax.sharding import Mesh, PartitionSpec as P

K = 512
S = 512
LEAF = 2048
NEWTON = 6
F32 = jnp.float32
BF16 = jnp.bfloat16
HIGH = lax.Precision.HIGH


def hop(block, axis, first):
    masks = (1, 3) if first else (3, 1)
    route = []
    for core in range(2):
        for place in range(4):
            route.append((core * 4 + place, core * 4 + (place ^ masks[core])))
    return lax.ppermute(block, ("core", axis), route)


def swapped(block, axis, mask):
    count = lax.axis_size(axis)
    return lax.ppermute(block, axis, [(i, i ^ mask) for i in range(count)])


def split3(value):
    high = lax.reduce_precision(value, 8, 7)
    rest = value - high
    middle = lax.reduce_precision(rest, 8, 7)
    return jnp.concatenate([high, middle, rest - middle], 0).astype(BF16)


def pick(value, order, kept):
    rows, length = value.shape
    place = lax.broadcasted_iota(jnp.int32, (length, order.shape[0]), 0)
    chosen = ((place == order[None, :]) & kept[None, :]).astype(BF16)
    parts = jnp.dot(split3(value), chosen, preferred_element_type=F32)
    return parts[:rows] + parts[rows : 2 * rows] + parts[2 * rows :]


def solve(skeleton, redundant):
    both = jnp.concatenate([skeleton, redundant], 1)
    products = lax.dot_general(
        both, skeleton, (((0,), (0,)), ((), ())), precision=HIGH, preferred_element_type=F32
    )
    identity = jnp.eye(K, dtype=F32)
    gram = products[:K] / (8.0 * S) + identity
    bound = jnp.max(jnp.sum(jnp.abs(gram), axis=0))
    power = identity - gram / bound
    out = products[K:] / (math.sqrt(S) * bound)
    for step in range(NEWTON):
        if step < NEWTON - 1:
            grown = jnp.dot(
                jnp.concatenate([power, out], 0), power, precision=HIGH, preferred_element_type=F32
            )
            power = grown[:K]
            out = out + grown[K:]
        else:
            out = out + jnp.dot(out, power, precision=HIGH, preferred_element_type=F32)
    return out


def local(a_matrix, omega, leaf_pivots, upper_pivots, ranks):
    z, core, y, x = (lax.axis_index(name) for name in ("z", "core", "y", "x"))
    slots = jnp.where(core == 0, jnp.array([0, 3, 1, 2]), jnp.array([0, 1, 3, 2]))

    new = lax.broadcasted_iota(jnp.int32, (2, 4, 4, 16), 3)
    first = slots[None, :, None, None]
    second = slots[None, None, :, None]
    half_a = ((x ^ first) * 4 + (y ^ second)) * 16
    half_b = ((x ^ second) * 4 + (y ^ first)) * 16 + 256
    half = lax.broadcasted_iota(jnp.int32, (2, 4, 4, 16), 0)
    old = (jnp.where(half == 0, half_a, half_b) + new).reshape(S)
    chosen = (old[:, None] == lax.broadcasted_iota(jnp.int32, (S, S), 1)).astype(BF16)
    omega_t = lax.dot_general(
        chosen, omega, (((1,), (1,)), ((), ())), preferred_element_type=F32
    ).astype(BF16)

    def partial_rows(low, count):
        return lax.dot_general(
            omega_t[low : low + count],
            a_matrix,
            (((1,), (1,)), ((), ())),
            preferred_element_type=F32,
        )

    send_a, send_b = partial_rows(128, 128), partial_rows(384, 128)
    got_a, got_b = hop(send_a, "x", True), hop(send_b, "y", True)
    keep_a, keep_b = partial_rows(0, 128), partial_rows(256, 128)
    sum_a, sum_b = keep_a + got_a, keep_b + got_b
    got_a, got_b = hop(sum_a[64:], "x", False), hop(sum_b[64:], "y", False)
    sum_a, sum_b = sum_a[:64] + got_a, sum_b[:64] + got_b
    got_a, got_b = hop(sum_a[32:], "y", True), hop(sum_b[32:], "x", True)
    sum_a, sum_b = sum_a[:32] + got_a, sum_b[:32] + got_b
    got_a, got_b = hop(sum_a[16:], "y", False), hop(sum_b[16:], "x", False)
    samples = jnp.concatenate([sum_a[:16] + got_a, sum_b[:16] + got_b], 0)

    def compress(rows, pivots, rank):
        kept = jnp.arange(pivots.shape[0]) < rank
        kept = kept | (jnp.arange(pivots.shape[0]) >= K)
        moved = pick(rows, pivots, kept)
        return moved[:, :K], moved[:, K:]

    row_index = z * 2 + core
    skeleton, leaf_redundant = compress(samples, leaf_pivots[0], ranks[0, row_index])
    leaf_skeleton = skeleton
    levels = []
    for level, axis, mask in ((1, "core", 1), (2, "z", 1), (3, "z", 2)):
        sibling = swapped(skeleton, axis, mask)
        side = row_index >> (level - 1) & 1
        rows = jnp.concatenate(
            [jnp.where(side == 0, skeleton, sibling), jnp.where(side == 0, sibling, skeleton)], 1
        )
        node = row_index >> level
        skeleton, redundant = compress(rows, upper_pivots[level - 1, node], ranks[level, node])
        levels.append(jnp.concatenate([skeleton, redundant], 1))

    odd = z & 1
    upper = jnp.where(core == 0, levels[0], jnp.where(odd == 0, levels[1], levels[2]))
    spread = jnp.concatenate(
        [
            jnp.broadcast_to(leaf_skeleton[None], (16, 32, K)),
            jnp.broadcast_to(upper[None, :, :K], (16, 32, K)),
            leaf_redundant.reshape(32, 16, 96).transpose(1, 0, 2),
            upper[:, K:].reshape(32, 16, 32).transpose(1, 0, 2),
        ],
        2,
    )
    whole = lax.all_to_all(spread, ("y", "x"), 0, 0, tiled=False).reshape(S, 2 * K + 128)
    leaf_interp = solve(whole[:, :K], whole[:, 2 * K : 2 * K + 96])
    upper_interp = solve(whole[:, K : 2 * K], whole[:, 2 * K + 96 :])

    other = swapped(upper_interp, "core", 1)
    level_1 = jnp.where(core == 0, upper_interp, other)
    chip = jnp.where(core == 0, other, upper_interp)
    beside = swapped(chip, "z", 1)
    level_2 = jnp.where(odd == 0, chip, beside)
    level_3 = jnp.where(odd == 0, beside, chip)
    return (leaf_interp[None], jnp.stack([level_1, level_2, level_3])[:, None])


def solution(mesh):
    grid = Mesh(mesh.devices.reshape(8, 2, 4, 4), ("z", "core", "y", "x"))
    row, col = ("z", "core"), ("y", "x")
    return jax.shard_map(
        local,
        mesh=grid,
        in_specs=(P(row, col), P(col, None), P(row, None), P(), P()),
        out_specs=(P(row, col, None), P(None, row, col, None)),
        check_vma=False,
    )
```

```python
import functools
import math

import jax
import jax.numpy as jnp
from jax import lax
from jax.experimental import pallas as pl
from jax.experimental.pallas import tpu as pltpu
from jax.sharding import Mesh, PartitionSpec as P

K = 512
S = 512
LEAF = 2048
NEWTON = 6
F32 = jnp.float32
BF16 = jnp.bfloat16


def hop(block, axis, first):
    masks = (1, 3) if first else (3, 1)
    route = []
    for core in range(2):
        for place in range(4):
            route.append((core * 4 + place, core * 4 + (place ^ masks[core])))
    return lax.ppermute(block, ("core", axis), route)


def swapped(block, axis, mask):
    count = lax.axis_size(axis)
    return lax.ppermute(block, axis, [(i, i ^ mask) for i in range(count)])


def split3(value):
    high = lax.reduce_precision(value, 8, 7)
    rest = value - high
    middle = lax.reduce_precision(rest, 8, 7)
    return jnp.concatenate([high, middle, rest - middle], 0).astype(BF16)


def pick(value, order, kept):
    rows, length = value.shape
    place = lax.broadcasted_iota(jnp.int32, (length, order.shape[0]), 0)
    chosen = ((place == order[None, :]) & kept[None, :]).astype(BF16)
    parts = jnp.dot(split3(value), chosen, preferred_element_type=F32)
    return parts[:rows] + parts[rows : 2 * rows] + parts[2 * rows :]


def ordered_kernel(place_ref, omega_ref, a_ref, out_a_ref, out_b_ref, lhs_ref, *, sent):
    @pl.when(pl.program_id(0) == 0)
    def _():
        x, y, core = place_ref[0], place_ref[1], place_ref[2]
        near = jnp.where(core == 0, 1, 3)
        far = jnp.where(core == 0, 3, 1)
        row = lax.broadcasted_iota(jnp.int32, (256, 1), 0)
        outer = (row >> 6) & 1
        if sent:
            first = jnp.where(outer == 0, near, 2)
        else:
            first = jnp.where(outer == 0, 0, far)
        inner = (row >> 4) & 3
        second = jnp.where(
            inner == 0, 0, jnp.where(inner == 1, far, jnp.where(inner == 2, near, 2))
        )
        half_a = (x ^ first) * 64 + (y ^ second) * 16
        half_b = (x ^ second) * 64 + (y ^ first) * 16 + 256
        old = jnp.where(row < 128, half_a, half_b) + (row & 15)
        place = lax.broadcasted_iota(jnp.int32, (256, S), 1)
        chosen = jnp.where(place == old, 1.0, 0.0).astype(BF16)
        lhs_ref[...] = lax.dot_general(
            chosen, omega_ref[...], (((1,), (1,)), ((), ())), preferred_element_type=F32
        ).astype(BF16)

    rows = lax.dot_general(
        lhs_ref[...], a_ref[...], (((1,), (1,)), ((), ())), preferred_element_type=F32
    )
    out_a_ref[...] = rows[:128]
    out_b_ref[...] = rows[128:]


def ordered_samples(place, omega, a_matrix, sent):
    depth = a_matrix.shape[1]
    block = 256
    out = jax.ShapeDtypeStruct((128, LEAF), F32)
    return pl.pallas_call(
        functools.partial(ordered_kernel, sent=sent),
        grid_spec=pltpu.PrefetchScalarGridSpec(
            num_scalar_prefetch=1,
            grid=(LEAF // block,),
            in_specs=[
                pl.BlockSpec((depth, S), lambda i, _: (0, 0)),
                pl.BlockSpec((block, depth), lambda i, _: (i, 0)),
            ],
            out_specs=[pl.BlockSpec((128, block), lambda i, _: (0, i))] * 2,
            scratch_shapes=[pltpu.VMEM((256, depth), BF16)],
        ),
        out_shape=[out, out],
        compiler_params=pltpu.CompilerParams(vmem_limit_bytes=32 * 2**20),
        cost_estimate=pl.CostEstimate(
            flops=2 * 256 * depth * (LEAF + S),
            bytes_accessed=2 * depth * (LEAF + S) + 4 * 256 * LEAF,
            transcendentals=0,
        ),
        name="sent_samples" if sent else "kept_samples",
    )(place, omega, a_matrix)


def parts2(value):
    high = value.astype(BF16)
    return high, (value - high.astype(F32)).astype(BF16)


def dot3(left, right, dims):
    left_high, left_low = parts2(left)
    right_high, right_low = right

    def one(u, v):
        return lax.dot_general(u, v, (dims, ((), ())), preferred_element_type=F32)

    return one(left_high, right_high) + (one(left_low, right_high) + one(left_high, right_low))


def solve_kernel(skeleton_ref, redundant_ref, out_ref):
    skeleton = skeleton_ref[...]
    parts = parts2(skeleton)
    over_samples = ((0,), (0,))
    plain = ((1,), (0,))
    rows = lax.broadcasted_iota(jnp.int32, (K, K), 0)
    columns = lax.broadcasted_iota(jnp.int32, (K, K), 1)
    identity = jnp.where(rows == columns, 1.0, 0.0)
    gram = dot3(skeleton, parts, over_samples) * (1.0 / (8.0 * S)) + identity
    cross = dot3(redundant_ref[...], parts, over_samples)
    sums = jnp.sum(jnp.abs(gram), axis=0, keepdims=True)
    bound = jnp.max(sums, axis=1, keepdims=True)
    power = identity - gram / bound
    out = cross / (math.sqrt(S) * bound)
    for step in range(NEWTON):
        parts = parts2(power)
        out = out + dot3(out, parts, plain)
        if step < NEWTON - 1:
            power = dot3(power, parts, plain)
    out_ref[...] = out


def solve(skeleton, redundant):
    rows = redundant.shape[1]
    return pl.pallas_call(
        solve_kernel,
        out_shape=jax.ShapeDtypeStruct((rows, K), F32),
        in_specs=[pl.BlockSpec(memory_space=pltpu.VMEM)] * 2,
        out_specs=pl.BlockSpec(memory_space=pltpu.VMEM),
        compiler_params=pltpu.CompilerParams(vmem_limit_bytes=40 * 2**20),
        cost_estimate=pl.CostEstimate(
            flops=6 * 6 * (K + rows) * K * K, bytes_accessed=4 * (S + rows) * K, transcendentals=0
        ),
        name="solve",
    )(skeleton, redundant)


def local(a_matrix, omega, leaf_pivots, upper_pivots, ranks):
    z, core, y, x = (lax.axis_index(name) for name in ("z", "core", "y", "x"))
    place = jnp.stack([x, y, core]).astype(jnp.int32)
    send_a, send_b = ordered_samples(place, omega, a_matrix, True)
    got_a, got_b = hop(send_a, "x", True), hop(send_b, "y", True)
    keep_a, keep_b = ordered_samples(place, omega, a_matrix, False)
    sum_a, sum_b = keep_a + got_a, keep_b + got_b
    got_a, got_b = hop(sum_a[64:], "x", False), hop(sum_b[64:], "y", False)
    sum_a, sum_b = sum_a[:64] + got_a, sum_b[:64] + got_b
    got_a, got_b = hop(sum_a[32:], "y", True), hop(sum_b[32:], "x", True)
    sum_a, sum_b = sum_a[:32] + got_a, sum_b[:32] + got_b
    got_a, got_b = hop(sum_a[16:], "y", False), hop(sum_b[16:], "x", False)
    samples = jnp.concatenate([sum_a[:16] + got_a, sum_b[:16] + got_b], 0)

    def compress(rows, pivots, rank):
        kept = jnp.arange(pivots.shape[0]) < rank
        kept = kept | (jnp.arange(pivots.shape[0]) >= K)
        moved = pick(rows, pivots, kept)
        return moved[:, :K], moved[:, K:]

    row_index = z * 2 + core
    skeleton, leaf_redundant = compress(samples, leaf_pivots[0], ranks[0, row_index])
    leaf_skeleton = skeleton
    levels = []
    for level, axis, mask in ((1, "core", 1), (2, "z", 1), (3, "z", 2)):
        sibling = swapped(skeleton, axis, mask)
        side = row_index >> (level - 1) & 1
        rows = jnp.concatenate(
            [jnp.where(side == 0, skeleton, sibling), jnp.where(side == 0, sibling, skeleton)], 1
        )
        node = row_index >> level
        skeleton, redundant = compress(rows, upper_pivots[level - 1, node], ranks[level, node])
        levels.append(jnp.concatenate([skeleton, redundant], 1))

    odd = z & 1
    upper = jnp.where(core == 0, levels[0], jnp.where(odd == 0, levels[1], levels[2]))
    spread = jnp.concatenate(
        [
            jnp.broadcast_to(leaf_skeleton[None], (16, 32, K)),
            jnp.broadcast_to(upper[None, :, :K], (16, 32, K)),
            leaf_redundant.reshape(32, 16, 96).transpose(1, 0, 2),
            upper[:, K:].reshape(32, 16, 32).transpose(1, 0, 2),
        ],
        2,
    )
    whole = lax.all_to_all(spread, ("y", "x"), 0, 0, tiled=False).reshape(S, 2 * K + 128)
    leaf_interp = solve(whole[:, :K], whole[:, 2 * K : 2 * K + 96])
    upper_interp = solve(whole[:, K : 2 * K], whole[:, 2 * K + 96 :])

    other = swapped(upper_interp, "core", 1)
    level_1 = jnp.where(core == 0, upper_interp, other)
    chip = jnp.where(core == 0, other, upper_interp)
    beside = swapped(chip, "z", 1)
    level_2 = jnp.where(odd == 0, chip, beside)
    level_3 = jnp.where(odd == 0, beside, chip)
    return (leaf_interp[None], jnp.stack([level_1, level_2, level_3])[:, None])


def solution(mesh):
    grid = Mesh(mesh.devices.reshape(8, 2, 4, 4), ("z", "core", "y", "x"))
    row, col = ("z", "core"), ("y", "x")
    return jax.shard_map(
        local,
        mesh=grid,
        in_specs=(P(row, col), P(col, None), P(row, None), P(), P()),
        out_specs=(P(row, col, None), P(None, row, col, None)),
        check_vma=False,
    )
```

```python
import functools
import math

import jax
import jax.numpy as jnp
from jax import lax
from jax.experimental import pallas as pl
from jax.experimental.pallas import tpu as pltpu
from jax.sharding import Mesh, PartitionSpec as P

K = 512
S = 512
LEAF = 2048
NEWTON = 6
F32 = jnp.float32
VMEM = pl.BlockSpec(memory_space=pltpu.VMEM)
ANY = pl.BlockSpec(memory_space=pl.ANY)
BF16 = jnp.bfloat16


def hop(block, axis, first):
    masks = (1, 3) if first else (3, 1)
    route = []
    for core in range(2):
        for place in range(4):
            route.append((core * 4 + place, core * 4 + (place ^ masks[core])))
    return lax.ppermute(block, ("core", axis), route)


def swapped(block, axis, mask):
    count = lax.axis_size(axis)
    return lax.ppermute(block, axis, [(i, i ^ mask) for i in range(count)])


def ordered_kernel(place_ref, omega_ref, a_ref, out_a_ref, out_b_ref, lhs_ref, *, sent):
    @pl.when(pl.program_id(0) == 0)
    def _():
        x, y, core = place_ref[0], place_ref[1], place_ref[2]
        near = jnp.where(core == 0, 1, 3)
        far = jnp.where(core == 0, 3, 1)
        row = lax.broadcasted_iota(jnp.int32, (256, 1), 0)
        outer = (row >> 6) & 1
        if sent:
            first = jnp.where(outer == 0, near, 2)
        else:
            first = jnp.where(outer == 0, 0, far)
        inner = (row >> 4) & 3
        second = jnp.where(
            inner == 0, 0, jnp.where(inner == 1, far, jnp.where(inner == 2, near, 2))
        )
        half_a = (x ^ first) * 64 + (y ^ second) * 16
        half_b = (x ^ second) * 64 + (y ^ first) * 16 + 256
        old = jnp.where(row < 128, half_a, half_b) + (row & 15)
        place = lax.broadcasted_iota(jnp.int32, (256, S), 1)
        chosen = jnp.where(place == old, 1.0, 0.0).astype(BF16)
        lhs_ref[...] = lax.dot_general(
            chosen, omega_ref[...], (((1,), (1,)), ((), ())), preferred_element_type=F32
        ).astype(BF16)

    rows = lax.dot_general(
        lhs_ref[...], a_ref[...], (((1,), (1,)), ((), ())), preferred_element_type=F32
    )
    out_a_ref[...] = rows[:128]
    out_b_ref[...] = rows[128:]


def ordered_samples(place, omega, a_matrix, sent):
    depth = a_matrix.shape[1]
    block = 1024
    out = jax.ShapeDtypeStruct((128, LEAF), F32)
    return pl.pallas_call(
        functools.partial(ordered_kernel, sent=sent),
        grid_spec=pltpu.PrefetchScalarGridSpec(
            num_scalar_prefetch=1,
            grid=(LEAF // block,),
            in_specs=[
                pl.BlockSpec((depth, S), lambda i, _: (0, 0)),
                pl.BlockSpec((block, depth), lambda i, _: (i, 0)),
            ],
            out_specs=[pl.BlockSpec((128, block), lambda i, _: (0, i))] * 2,
            scratch_shapes=[pltpu.VMEM((256, depth), BF16)],
        ),
        out_shape=[out, out],
        compiler_params=pltpu.CompilerParams(vmem_limit_bytes=56 * 2**20),
        cost_estimate=pl.CostEstimate(
            flops=2 * 256 * depth * (LEAF + S),
            bytes_accessed=2 * depth * (LEAF + S) + 4 * 256 * LEAF,
            transcendentals=0,
        ),
        name="sent_samples" if sent else "kept_samples",
    )(place, omega, a_matrix)


def parts2(value):
    high = value.astype(BF16)
    return high, (value - high.astype(F32)).astype(BF16)


def product(left, right):
    return jnp.dot(left, right, preferred_element_type=F32)


def solve_kernel(*refs, packed):
    out_ref = refs[-1]
    if packed:
        own_ref, got_ref = refs[:2]
        skeleton = jnp.concatenate([own_ref[:, :K], got_ref[:, :K]], 0)
        pieces = [own_ref[:128], own_ref[128:], got_ref[:128], got_ref[128:]]
        redundant = jnp.concatenate(
            [
                piece[:, K + 32 * slot : K + 32 * slot + 32]
                for piece, slot in zip(pieces, (0, 2, 1, 3))
            ],
            0,
        )
    else:
        own_ref, rest_ref, got_ref = refs[:3]
        skeleton = jnp.concatenate([own_ref[:, :K], got_ref[:, :K]], 0)
        redundant = jnp.concatenate([rest_ref[:, :96], got_ref[:, K : K + 96]], 0)
    count = redundant.shape[1]
    identity = jnp.where(
        lax.broadcasted_iota(jnp.int32, (K, K), 0) == lax.broadcasted_iota(jnp.int32, (K, K), 1),
        1.0,
        0.0,
    )

    def times(square, rows, high, low):
        rows_high, rows_low = parts2(rows)
        left = [rows_high, rows_low] if square is None else [square, rows_high, rows_low]
        first = product(jnp.concatenate(left, 0), high)
        second = product(jnp.concatenate(left[:-1], 0), low)
        start = 0 if square is None else K
        moved = (second[start:] + first[start + count :]) + first[start : start + count]
        if square is None:
            return None, moved
        mixed = second[:K]
        return first[:K] + (mixed + mixed.T), moved

    high, low = parts2(skeleton)
    gram, cross = times(parts2(skeleton.T)[0], redundant.T, high, low)
    gram = gram * (1.0 / (8.0 * S)) + identity
    bound = jnp.max(jnp.sum(jnp.abs(gram), axis=0, keepdims=True), axis=1, keepdims=True)
    power = identity - gram / bound
    out = cross / (math.sqrt(S) * bound)
    for step in range(NEWTON):
        high, low = parts2(power)
        power, moved = times(high if step < NEWTON - 1 else None, out, high, low)
        out = out + moved
    out_ref[...] = out


def solve(whole, rows, packed, after=()):
    return pl.pallas_call(
        functools.partial(solve_kernel, packed=packed),
        out_shape=jax.ShapeDtypeStruct((rows, K), F32),
        in_specs=[VMEM] * len(whole) + [ANY] * len(after),
        out_specs=VMEM,
        compiler_params=pltpu.CompilerParams(vmem_limit_bytes=24 * 2**20),
        cost_estimate=pl.CostEstimate(
            flops=6 * 6 * (K + rows) * K * K, bytes_accessed=4 * (S + rows) * K, transcendentals=0
        ),
        name="solve_upper" if packed else "solve_leaf",
    )(*whole, *after)


def add_kernel(kept_a, got_a, kept_b, got_b, out_a, out_b, *, first):
    rows = out_a.shape[0]
    part = slice(first, first + rows)
    out_a[...] = kept_a[part] + got_a[part]
    out_b[...] = kept_b[part] + got_b[part]


def added(kept, got, first, name):
    rows = kept[0].shape[0] // 2
    out = jax.ShapeDtypeStruct((rows, LEAF), F32)
    return pl.pallas_call(
        functools.partial(add_kernel, first=first),
        in_specs=[VMEM] * 4,
        out_specs=[VMEM] * 2,
        out_shape=[out, out],
        compiler_params=pltpu.CompilerParams(vmem_limit_bytes=16 * 2**20),
        cost_estimate=pl.CostEstimate(
            flops=2 * rows * LEAF, bytes_accessed=24 * rows * LEAF, transcendentals=0
        ),
        name=name,
    )(kept[0], got[0], kept[1], got[1])


def parts3(value):
    high = value.astype(BF16)
    rest = value - high.astype(F32)
    middle = rest.astype(BF16)
    low = (rest - middle.astype(F32)).astype(BF16)
    return jnp.concatenate([high, middle, low], 0)


def picked(parts, order):
    place = lax.broadcasted_iota(jnp.int32, (parts.shape[1], order.shape[1]), 0)
    chosen = jnp.where(place == order, 1.0, 0.0).astype(BF16)
    moved = jnp.dot(parts, chosen, preferred_element_type=F32)
    return (moved[:32] + moved[32:64]) + moved[64:]


def finish_kernel(order_ref, *refs):
    terms, (skeleton_ref, parts_ref) = refs[:-2], refs[-2:]
    half = len(terms) // 2
    totals = []
    for group in (terms[:half], terms[half:]):
        total = group[0][:16]
        for term in group[1:]:
            total = total + term[:16]
        totals.append(total)
    parts = parts3(jnp.concatenate(totals, 0))
    parts_ref[...] = parts
    skeleton_ref[...] = picked(parts, order_ref[...])


def finished(order, terms_a, terms_b):
    terms = [*terms_a, *terms_b]
    return pl.pallas_call(
        finish_kernel,
        in_specs=[VMEM] * (1 + len(terms)),
        out_specs=[VMEM] * 2,
        out_shape=[
            jax.ShapeDtypeStruct((32, K), F32),
            jax.ShapeDtypeStruct((96, LEAF), BF16),
        ],
        compiler_params=pltpu.CompilerParams(vmem_limit_bytes=16 * 2**20),
        cost_estimate=pl.CostEstimate(
            flops=2 * 96 * LEAF * K, bytes_accessed=4 * 16 * len(terms) * LEAF, transcendentals=0
        ),
        name="finish_samples",
    )(order, *terms)


def call(kernel, name, inputs, shapes, after=(), flops=10**6):
    return pl.pallas_call(
        kernel,
        in_specs=[VMEM] * len(inputs) + [ANY] * len(after),
        out_specs=[VMEM] * len(shapes),
        out_shape=[jax.ShapeDtypeStruct(shape, F32) for shape in shapes],
        compiler_params=pltpu.CompilerParams(vmem_limit_bytes=16 * 2**20),
        cost_estimate=pl.CostEstimate(flops=flops, bytes_accessed=10**6, transcendentals=0),
        name=name,
    )(*inputs, *after)


def leaf_kernel(order_ref, parts_ref, skeleton_ref, _, payload_ref, rest_ref):
    parts = parts_ref[...]
    payload_ref[:, :K] = skeleton_ref[...]
    for i in range(4):
        part = slice(i * K, i * K + K)
        moved = picked(parts, order_ref[:, part])
        if i < 2:
            rest_ref[:, part] = moved
        else:
            payload_ref[:, (i - 1) * K : i * K] = moved


def pack(own, rest, got, payload_ref, rest_ref):
    rows, half = own.shape[0], rest.shape[1] // 2
    payload_ref[:rows, :K] = own[:, :K]
    payload_ref[rows:, :K] = got[:, :K]
    payload_ref[:rows, K:] = rest[:, half:]
    payload_ref[rows:, K:] = got[:, K + half :]
    rest_ref[:rows] = rest[:, :half]
    rest_ref[rows:] = got[:, K : K + half]


def pack_kernel(own, rest, got, payload_ref, rest_ref):
    pack(own, rest, got, payload_ref, rest_ref)


def pack_all_kernel(own, rest, got, payload_ref):
    rows = own.shape[0]
    payload_ref[:rows, :K] = own[:, :K]
    payload_ref[:rows, K:] = rest[...]
    payload_ref[rows:] = got[...]


def stack_kernel(own, got, payload_ref):
    rows = own.shape[0]
    payload_ref[:rows] = own[...]
    payload_ref[rows:] = got[...]


def level_1_kernel(order, own, sibling, skeleton_ref, redundant_ref):
    moved = picked(parts3(jnp.concatenate([own[...], sibling[...]], 1)), order[...])
    skeleton_ref[...] = moved[:, :K]
    redundant_ref[...] = moved[:, K:]


def level_2_kernel(
    order, own, sibling, leaf, rest, got, skeleton_ref, redundant_ref, payload_ref, rest_ref
):
    level_1_kernel(order, own, sibling, skeleton_ref, redundant_ref)
    pack(leaf, rest, got, payload_ref, rest_ref)


def level_3_kernel(
    order, own, sibling, leaf, rest, got, which, skeleton_1, redundant_1, redundant_2,
    upper_ref, upper_rest_ref, payload_ref, rest_ref,
):
    moved = picked(parts3(jnp.concatenate([own[...], sibling[...]], 1)), order[...])
    first, second = which[0, 0] == 0, which[0, 0] == 1
    skeleton = jnp.where(first, skeleton_1[...], jnp.where(second, own[...], moved[:, :K]))
    redundant = jnp.where(first, redundant_1[...], jnp.where(second, redundant_2[...], moved[:, K:]))
    upper_ref[:, :K] = skeleton
    upper_ref[:, K:] = redundant[:, 256:]
    upper_rest_ref[...] = redundant[:, :256]
    pack(leaf, rest, got, payload_ref, rest_ref)


def local(a_matrix, omega, leaf_pivots, upper_pivots, ranks):
    z, core, y, x = (lax.axis_index(name) for name in ("z", "core", "y", "x"))
    row_index = z * 2 + core
    place = jnp.stack([x, y, core]).astype(jnp.int32)

    near = jnp.where(core == 0, 1, 3)
    far = 4 - near
    bit = [jnp.arange(16) >> i & 1 for i in (3, 2, 1, 0)]
    leaf_owners = ((y ^ bit[1] * near ^ bit[3] * far) * 4 + (x ^ bit[0] * near ^ bit[2] * far))
    upper_owners = ((y ^ bit[0] * near ^ bit[3] * far) * 4 + (x ^ bit[1] * near ^ bit[2] * far))
    position = jnp.arange(K)
    leaf_order = jnp.where(position < ranks[0, row_index], leaf_pivots[0, :K], -1)[None]
    leaf_rest = jnp.take(leaf_pivots[0, K:].reshape(16, 96), leaf_owners, axis=0)
    leaf_rest = jnp.pad(leaf_rest, ((0, 0), (0, 32)), constant_values=-1).reshape(1, LEAF)
    orders = []
    for level in (1, 2, 3):
        node, side = row_index >> level, row_index >> (level - 1) & 1
        pivots = upper_pivots[level - 1, node] ^ (side << 9)
        kept = jnp.where(position < ranks[level, node], pivots[:K], -1)
        rest = jnp.take(pivots[K:].reshape(16, 32), upper_owners, axis=0).reshape(K)
        orders.append(jnp.concatenate([kept, rest])[None])

    send = ordered_samples(place, omega, a_matrix, True)
    got = hop(send[0], "x", True), hop(send[1], "y", True)
    kept = ordered_samples(place, omega, a_matrix, False)
    for axes, first in (("xy", False), ("yx", True), ("yx", False)):
        send = added(kept, got, kept[0].shape[0] // 2, "add_sent")
        kept = added(kept, got, 0, "add_kept")
        got = hop(send[0], axes[0], first), hop(send[1], axes[1], first)
    leaf_skeleton, parts = finished(leaf_order, (kept[0], got[0]), (kept[1], got[1]))

    small = (32, K)
    sibling = swapped(leaf_skeleton, "core", 1)
    skeleton_1, redundant_1 = call(
        level_1_kernel, "level_1", (orders[0], leaf_skeleton, sibling), (small, small)
    )
    sibling = swapped(skeleton_1, "z", 1)
    leaf, rest = call(
        leaf_kernel,
        "leaf_redundant",
        (leaf_rest, parts, leaf_skeleton),
        ((32, 3 * K), (32, 2 * K)),
        (skeleton_1,),
    )
    got = hop(leaf, "x", True)
    skeleton_2, redundant_2, leaf, rest = call(
        level_2_kernel,
        "level_2",
        (orders[1], skeleton_1, sibling, leaf, rest, got),
        (small, small, (64, 2 * K), (64, K)),
    )
    inner = (z ^ z >> 1) & 1
    sibling = lax.ppermute(skeleton_2, "z", [(i, i ^ 3) for i in (1, 2, 5, 6)])
    got = hop(leaf, "y", True)
    which = jnp.broadcast_to(jnp.where(core == 0, 0, 1 + inner), (1, 128)).astype(jnp.int32)
    upper, upper_rest, leaf, rest = call(
        level_3_kernel,
        "level_3",
        (orders[2], skeleton_2, sibling, leaf, rest, got, which)
        + (skeleton_1, redundant_1, redundant_2),
        ((32, K + 256), (32, 256), (128, K + 256), (128, 256)),
    )
    upper_got = hop(upper, "y", True)
    got = hop(leaf, "x", False)
    upper, upper_rest = call(
        pack_kernel, "upper_2", (upper, upper_rest, upper_got), ((64, K + 128), (64, 128))
    )
    upper_got = hop(upper, "x", True)
    leaf, rest = call(pack_kernel, "leaf_4", (leaf, rest, got), ((256, K + 128), (256, 128)))
    got = hop(leaf, "y", False)
    (upper,) = call(pack_all_kernel, "upper_3", (upper, upper_rest, upper_got), ((128, K + 128),))
    upper_got = hop(upper, "x", False)
    (upper,) = call(stack_kernel, "upper_4", (upper, upper_got), ((256, K + 128),))
    upper_got = hop(upper, "y", False)
    leaf_interp = solve((leaf, rest, got), 96, False)
    upper_interp = solve((upper, upper_got), 32, True, (leaf_interp,))

    other = swapped(upper_interp, "core", 1)
    level_1 = jnp.where(core == 0, upper_interp, other)
    chip = jnp.where(core == 0, other, upper_interp)
    beside = swapped(chip, "z", 1)
    level_2 = jnp.where(inner == 0, chip, beside)
    level_3 = jnp.where(inner == 0, beside, chip)
    return (leaf_interp[None], jnp.stack([level_1, level_2, level_3])[:, None])


def solution(mesh):
    grid = Mesh(mesh.devices.reshape(8, 2, 4, 4), ("z", "core", "y", "x"))
    row, col = ("z", "core"), ("y", "x")
    return jax.shard_map(
        local,
        mesh=grid,
        in_specs=(P(row, col), P(col, None), P(row, None), P(), P()),
        out_specs=(P(row, col, None), P(None, row, col, None)),
        check_vma=False,
    )
```

```python
import functools
import math

import jax
import jax.numpy as jnp
from jax import lax
from jax.experimental import pallas as pl
from jax.experimental.pallas import tpu as pltpu
from jax.sharding import Mesh, PartitionSpec as P

K = 512
S = 512
LEAF = 2048
NEWTON = 6
F32 = jnp.float32
VMEM = pl.BlockSpec(memory_space=pltpu.VMEM)
ANY = pl.BlockSpec(memory_space=pl.ANY)
BF16 = jnp.bfloat16


def hop(block, axis, first):
    masks = (1, 3) if first else (3, 1)
    route = []
    for core in range(2):
        for place in range(4):
            route.append((core * 4 + place, core * 4 + (place ^ masks[core])))
    return lax.ppermute(block, ("core", axis), route)


def swapped(block, axis, mask):
    count = lax.axis_size(axis)
    return lax.ppermute(block, axis, [(i, i ^ mask) for i in range(count)])


def ordered_kernel(omega_ref, a_ref, *refs, sent):
    lhs_ref = refs[4]

    @pl.when(pl.program_id(0) == 0)
    def _():
        x, y, core = (lax.axis_index(name) for name in ("x", "y", "core"))
        near = jnp.where(core == 0, 1, 3)
        far = jnp.where(core == 0, 3, 1)
        row = lax.broadcasted_iota(jnp.int32, (256, 1), 0)
        outer = (row >> 6) & 1
        if sent:
            first = jnp.where(outer == 0, near, 2)
        else:
            first = jnp.where(outer == 0, 0, far)
        inner = (row >> 4) & 3
        second = jnp.where(
            inner == 0, 0, jnp.where(inner == 1, far, jnp.where(inner == 2, near, 2))
        )
        half_a = (x ^ first) * 64 + (y ^ second) * 16
        half_b = (x ^ second) * 64 + (y ^ first) * 16 + 256
        old = jnp.where(row < 128, half_a, half_b) + (row & 15)
        place = lax.broadcasted_iota(jnp.int32, (256, S), 1)
        chosen = jnp.where(place == old, 1.0, 0.0).astype(BF16)
        lhs_ref[...] = lax.dot_general(
            chosen, omega_ref[...], (((1,), (1,)), ((), ())), preferred_element_type=F32
        ).astype(BF16)

    rows = lax.dot_general(
        lhs_ref[...], a_ref[...], (((1,), (1,)), ((), ())), preferred_element_type=F32
    )
    for i in range(4):
        refs[i][...] = rows[64 * i : 64 * i + 64]


def ordered_samples(omega, a_matrix, sent):
    depth = a_matrix.shape[1]
    block = 1024
    out = jax.ShapeDtypeStruct((64, LEAF), F32)
    return pl.pallas_call(
        functools.partial(ordered_kernel, sent=sent),
        grid=(LEAF // block,),
        in_specs=[
            pl.BlockSpec((depth, S), lambda i: (0, 0)),
            pl.BlockSpec((block, depth), lambda i: (i, 0)),
        ],
        out_specs=[pl.BlockSpec((64, block), lambda i: (0, i))] * 4,
        scratch_shapes=[pltpu.VMEM((256, depth), BF16)],
        out_shape=[out] * 4,
        compiler_params=pltpu.CompilerParams(vmem_limit_bytes=(56 if sent else 16) * 2**20),
        cost_estimate=pl.CostEstimate(
            flops=2 * 256 * depth * (LEAF + S),
            bytes_accessed=2 * depth * (LEAF + S) + 4 * 256 * LEAF,
            transcendentals=0,
        ),
        name="sent_samples" if sent else "kept_samples",
    )(omega, a_matrix)


def parts2(value):
    high = value.astype(BF16)
    return high, (value - high.astype(F32)).astype(BF16)


def product(left, right):
    return jnp.dot(left, right, preferred_element_type=F32)


def solve_kernel(*refs, packed):
    out_ref = refs[-2]
    refs[-1][...] = jnp.zeros_like(refs[-1])
    if packed:
        pieces = refs[:4]
        skeleton = jnp.concatenate([piece[:, :K] for piece in pieces], 0)
        redundant = jnp.concatenate(
            [
                piece[:, K + 32 * slot : K + 32 * slot + 32]
                for piece, slot in zip(pieces, (0, 2, 1, 3))
            ],
            0,
        )
    else:
        own_ref, rest_ref, got_ref = refs[:3]
        skeleton = jnp.concatenate([own_ref[:, :K], got_ref[:, :K]], 0)
        redundant = jnp.concatenate([rest_ref[:, :96], got_ref[:, K : K + 96]], 0)
    count = redundant.shape[1]
    identity = jnp.where(
        lax.broadcasted_iota(jnp.int32, (K, K), 0) == lax.broadcasted_iota(jnp.int32, (K, K), 1),
        1.0,
        0.0,
    )

    def times(square, rows, high, low):
        rows_high, rows_low = parts2(rows)
        left = [rows_high, rows_low] if square is None else [square, rows_high, rows_low]
        first = product(jnp.concatenate(left, 0), high)
        second = product(jnp.concatenate(left[:-1], 0), low)
        start = 0 if square is None else K
        moved = (second[start:] + first[start + count :]) + first[start : start + count]
        if square is None:
            return None, moved
        mixed = second[:K]
        return first[:K] + (mixed + mixed.T), moved

    high, low = parts2(skeleton)
    gram, cross = times(parts2(skeleton.T)[0], redundant.T, high, low)
    gram = gram * (1.0 / (8.0 * S)) + identity
    bound = jnp.max(jnp.sum(jnp.abs(gram), axis=0, keepdims=True), axis=1, keepdims=True)
    power = identity - gram / bound
    out = cross / (math.sqrt(S) * bound)
    for step in range(NEWTON):
        high, low = parts2(power)
        power, moved = times(high if step < NEWTON - 1 else None, out, high, low)
        out = out + moved
    out_ref[...] = out


def solve(whole, rows, packed, after=()):
    return pl.pallas_call(
        functools.partial(solve_kernel, packed=packed),
        out_shape=[jax.ShapeDtypeStruct(shape, F32) for shape in ((rows, K), (8, 128))],
        in_specs=[VMEM] * len(whole) + [ANY] * len(after),
        out_specs=[VMEM] * 2,
        compiler_params=pltpu.CompilerParams(vmem_limit_bytes=24 * 2**20),
        cost_estimate=pl.CostEstimate(
            flops=6 * 6 * (K + rows) * K * K, bytes_accessed=4 * (S + rows) * K, transcendentals=0
        ),
        name="solve_upper" if packed else "solve_leaf",
    )(*whole, *after)


def add_kernel(kept_a, got_a, kept_b, got_b, out_a, out_b, *, first):
    rows = out_a.shape[0]
    part = slice(first, first + rows)
    out_a[...] = kept_a[part] + got_a[part]
    out_b[...] = kept_b[part] + got_b[part]


def added(kept, got, first, rows, name):
    out = jax.ShapeDtypeStruct((rows, LEAF), F32)
    return pl.pallas_call(
        functools.partial(add_kernel, first=first),
        in_specs=[VMEM] * 4,
        out_specs=[VMEM] * 2,
        out_shape=[out, out],
        compiler_params=pltpu.CompilerParams(vmem_limit_bytes=16 * 2**20),
        cost_estimate=pl.CostEstimate(
            flops=2 * rows * LEAF, bytes_accessed=24 * rows * LEAF, transcendentals=0
        ),
        name=name,
    )(kept[0], got[0], kept[1], got[1])


def parts3(value):
    high = value.astype(BF16)
    rest = value - high.astype(F32)
    middle = rest.astype(BF16)
    low = (rest - middle.astype(F32)).astype(BF16)
    return jnp.concatenate([high, middle, low], 0)


def picked(parts, order):
    place = lax.broadcasted_iota(jnp.int32, (parts.shape[1], order.shape[1]), 0)
    chosen = jnp.where(place == order, 1.0, 0.0).astype(BF16)
    moved = jnp.dot(parts, chosen, preferred_element_type=F32)
    return (moved[:32] + moved[32:64]) + moved[64:]


def finish_kernel(order_ref, *refs):
    terms, (skeleton_ref, parts_ref) = refs[:4], refs[-2:]
    half = len(terms) // 2
    totals = []
    for group in (terms[:half], terms[half:]):
        total = group[0][:16]
        for term in group[1:]:
            total = total + term[:16]
        totals.append(total)
    parts = parts3(jnp.concatenate(totals, 0))
    parts_ref[...] = parts
    skeleton_ref[...] = picked(parts, order_ref[...])


def finished(order, terms_a, terms_b, after):
    terms = [*terms_a, *terms_b]
    return pl.pallas_call(
        finish_kernel,
        in_specs=[VMEM] * (1 + len(terms)) + [ANY] * len(after),
        out_specs=[VMEM] * 2,
        out_shape=[
            jax.ShapeDtypeStruct((32, K), F32),
            jax.ShapeDtypeStruct((96, LEAF), BF16),
        ],
        compiler_params=pltpu.CompilerParams(vmem_limit_bytes=16 * 2**20),
        cost_estimate=pl.CostEstimate(
            flops=2 * 96 * LEAF * K, bytes_accessed=4 * 16 * len(terms) * LEAF, transcendentals=0
        ),
        name="finish_samples",
    )(order, *terms, *after)


def call(kernel, name, inputs, shapes, after=(), flops=10**6):
    return pl.pallas_call(
        kernel,
        in_specs=[VMEM] * len(inputs) + [ANY] * len(after),
        out_specs=[VMEM] * len(shapes),
        out_shape=[jax.ShapeDtypeStruct(shape, F32) for shape in shapes],
        compiler_params=pltpu.CompilerParams(vmem_limit_bytes=16 * 2**20),
        cost_estimate=pl.CostEstimate(flops=flops, bytes_accessed=10**6, transcendentals=0),
        name=name,
    )(*inputs, *after)


def leaf_kernel(order_ref, parts_ref, skeleton_ref, payload_ref, rest_ref):
    parts = parts_ref[...]
    payload_ref[:, :K] = skeleton_ref[...]
    for i in range(4):
        part = slice(i * K, i * K + K)
        moved = picked(parts, order_ref[:, part])
        if i < 2:
            rest_ref[:, part] = moved
        else:
            payload_ref[:, (i - 1) * K : i * K] = moved


def pack(own, rest, got, payload_ref, rest_ref):
    rows, half = own.shape[0], rest.shape[1] // 2
    payload_ref[:rows, :K] = own[:, :K]
    payload_ref[rows:, :K] = got[:, :K]
    payload_ref[:rows, K:] = rest[:, half:]
    payload_ref[rows:, K:] = got[:, K + half :]
    rest_ref[:rows] = rest[:, :half]
    rest_ref[rows:] = got[:, K : K + half]


def pack_kernel(own, rest, got, *refs):
    pack(own, rest, got, *refs[-2:])


def pack_all_kernel(own, rest, got, payload_ref):
    rows = own.shape[0]
    payload_ref[:rows, :K] = own[:, :K]
    payload_ref[:rows, K:] = rest[...]
    payload_ref[rows:] = got[...]


def level_1_kernel(order, own, sibling, skeleton_ref, redundant_ref):
    moved = picked(parts3(jnp.concatenate([own[...], sibling[...]], 1)), order[...])
    skeleton_ref[...] = moved[:, :K]
    redundant_ref[...] = moved[:, K:]


def level_2_kernel(order, own, sibling, leaf, skeleton_ref, redundant_ref, payload_ref):
    level_1_kernel(order, own, sibling, skeleton_ref, redundant_ref)
    payload_ref[...] = leaf[...]


def level_3_kernel(
    order, own, sibling, leaf, rest, got, which, skeleton_1, redundant_1, redundant_2,
    upper_ref, upper_rest_ref, payload_ref, rest_ref,
):
    moved = picked(parts3(jnp.concatenate([own[...], sibling[...]], 1)), order[...])
    first, second = which[0, 0] == 0, which[0, 0] == 1
    skeleton = jnp.where(first, skeleton_1[...], jnp.where(second, own[...], moved[:, :K]))
    redundant = jnp.where(first, redundant_1[...], jnp.where(second, redundant_2[...], moved[:, K:]))
    upper_ref[:, :K] = skeleton
    upper_ref[:, K:] = redundant[:, 256:]
    upper_rest_ref[...] = redundant[:, :256]
    pack(leaf, rest, got, payload_ref, rest_ref)


def local(a_matrix, omega, leaf_pivots, upper_pivots, ranks):
    z, core, y, x = (lax.axis_index(name) for name in ("z", "core", "y", "x"))
    row_index = z * 2 + core

    near = jnp.where(core == 0, 1, 3)
    far = 4 - near
    bit = [jnp.arange(16) >> i & 1 for i in (3, 2, 1, 0)]
    leaf_owners = (y ^ bit[2] * near ^ bit[3] * far) * 4 + (x ^ bit[0] * near ^ bit[1] * far)
    upper_owners = (y ^ bit[0] * near ^ bit[3] * far) * 4 + (x ^ bit[1] * near ^ bit[2] * far)
    position = jnp.arange(K)
    leaf_order = jnp.where(position < ranks[0, row_index], leaf_pivots[0, :K], -1)[None]
    leaf_rest = jnp.take(leaf_pivots[0, K:].reshape(16, 96), leaf_owners, axis=0)
    leaf_rest = jnp.pad(leaf_rest, ((0, 0), (0, 32)), constant_values=-1).reshape(1, LEAF)
    orders = []
    for level in (1, 2, 3):
        node, side = row_index >> level, row_index >> (level - 1) & 1
        pivots = upper_pivots[level - 1, node] ^ (side << 9)
        head = jnp.where(position < ranks[level, node], pivots[:K], -1)
        rest = jnp.take(pivots[K:].reshape(16, 32), upper_owners, axis=0).reshape(K)
        orders.append(jnp.concatenate([head, rest])[None])

    near_a, both_a, near_b, both_b = ordered_samples(omega, a_matrix, True)
    got_both = hop(both_a, "x", True), hop(both_b, "y", True)
    got_near = hop(near_a, "x", True), hop(near_b, "y", True)
    own_a, far_a, own_b, far_b = ordered_samples(omega, a_matrix, False)
    send = added((far_a, far_b), got_both, 0, 64, "add_sent")
    got = hop(send[0], "x", False), hop(send[1], "y", False)
    kept = added((own_a, own_b), got_near, 0, 64, "add_kept")

    for rows, first in ((32, True), (16, False)):
        send = added(kept, got, rows, rows, "add_sent")
        kept = added(kept, got, 0, rows, "add_kept")
        got = hop(send[0], "y", first), hop(send[1], "x", first)
    leaf_skeleton, parts = finished(leaf_order, (kept[0], got[0]), (kept[1], got[1]), orders)

    small = (32, K)
    sibling = swapped(leaf_skeleton, "core", 1)
    skeleton_1, redundant_1 = call(
        level_1_kernel, "level_1", (orders[0], leaf_skeleton, sibling), (small, small)
    )
    sibling = swapped(skeleton_1, "z", 1)
    leaf, rest = call(
        leaf_kernel,
        "leaf_redundant",
        (leaf_rest, parts, leaf_skeleton),
        ((32, 3 * K), (32, 2 * K)),
        flops=2 * 96 * LEAF * LEAF,
    )
    skeleton_2, redundant_2, leaf = call(
        level_2_kernel,
        "level_2",
        (orders[1], skeleton_1, sibling, leaf),
        (small, small, (32, 3 * K)),
    )
    inner = (z ^ z >> 1) & 1
    sibling = lax.ppermute(skeleton_2, "z", [(i, i ^ 3) for i in (1, 2, 5, 6)])
    got = hop(leaf, "x", True)
    which = jnp.broadcast_to(jnp.where(core == 0, 0, 1 + inner), (1, 128)).astype(jnp.int32)
    upper, upper_rest, leaf, rest = call(
        level_3_kernel,
        "level_3",
        (orders[2], skeleton_2, sibling, leaf, rest, got, which)
        + (skeleton_1, redundant_1, redundant_2),
        ((32, K + 256), (32, 256), (64, 2 * K), (64, K)),
    )
    upper_got = hop(upper, "y", True)
    got = hop(leaf, "x", False)
    upper, upper_rest = call(
        pack_kernel, "upper_2", (upper, upper_rest, upper_got), ((64, K + 128), (64, 128))
    )
    upper_got = hop(upper, "x", True)
    leaf, rest = call(
        pack_kernel, "leaf_3", (leaf, rest, got), ((128, K + 256), (128, 256)), (upper,)
    )
    got = hop(leaf, "y", True)
    (upper,) = call(pack_all_kernel, "upper_3", (upper, upper_rest, upper_got), ((128, K + 128),))
    upper_got, across = hop(upper, "x", False), hop(upper, "y", False)
    leaf, rest = call(
        pack_kernel, "leaf_4", (leaf, rest, got), ((256, K + 128), (256, 128)), (upper,)
    )
    got = hop(leaf, "y", False)
    beyond = hop(upper_got, "y", False)
    leaf_interp, done = solve((leaf, rest, got), 96, False, (upper_got,))
    upper_interp, _ = solve((upper, upper_got, across, beyond), 32, True, (done,))

    other = swapped(upper_interp, "core", 1)
    level_1 = jnp.where(core == 0, upper_interp, other)
    chip = jnp.where(core == 0, other, upper_interp)
    beside = swapped(chip, "z", 1)
    level_2 = jnp.where(inner == 0, chip, beside)
    level_3 = jnp.where(inner == 0, beside, chip)
    return (leaf_interp[None], jnp.stack([level_1, level_2, level_3])[:, None])


def solution(mesh):
    grid = Mesh(mesh.devices.reshape(8, 2, 4, 4), ("z", "core", "y", "x"))
    row, col = ("z", "core"), ("y", "x")
    return jax.shard_map(
        local,
        mesh=grid,
        in_specs=(P(row, col), P(col, None), P(row, None), P(), P()),
        out_specs=(P(row, col, None), P(None, row, col, None)),
        check_vma=False,
    )
```

```python
import functools
import math

import jax
import jax.numpy as jnp
from jax import lax
from jax.experimental import pallas as pl
from jax.experimental.pallas import tpu as pltpu
from jax.sharding import Mesh, PartitionSpec as P

K = 512
S = 512
LEAF = 2048
NEWTON = 6
F32 = jnp.float32
VMEM = pl.BlockSpec(memory_space=pltpu.VMEM)
ANY = pl.BlockSpec(memory_space=pl.ANY)
BF16 = jnp.bfloat16


def hop(block, axis, first):
    masks = (1, 3) if first else (3, 1)
    route = []
    for core in range(2):
        for place in range(4):
            route.append((core * 4 + place, core * 4 + (place ^ masks[core])))
    return lax.ppermute(block, ("core", axis), route)


def swapped(block, axis, mask):
    count = lax.axis_size(axis)
    return lax.ppermute(block, axis, [(i, i ^ mask) for i in range(count)])


def ordered_kernel(omega_ref, a_ref, *refs, sent):
    lhs_ref = refs[4]

    @pl.when(pl.program_id(0) == 0)
    def _():
        x, y, core = (lax.axis_index(name) for name in ("x", "y", "core"))
        near = jnp.where(core == 0, 1, 3)
        far = jnp.where(core == 0, 3, 1)
        row = lax.broadcasted_iota(jnp.int32, (256, 1), 0)
        outer = (row >> 6) & 1
        if sent:
            first = jnp.where(outer == 0, near, 2)
        else:
            first = jnp.where(outer == 0, 0, far)
        inner = (row >> 4) & 3
        second = jnp.where(
            inner == 0, 0, jnp.where(inner == 1, far, jnp.where(inner == 2, near, 2))
        )
        half_a = (x ^ first) * 64 + (y ^ second) * 16
        half_b = (x ^ second) * 64 + (y ^ first) * 16 + 256
        old = jnp.where(row < 128, half_a, half_b) + (row & 15)
        place = lax.broadcasted_iota(jnp.int32, (256, S), 1)
        chosen = jnp.where(place == old, 1.0, 0.0).astype(BF16)
        lhs_ref[...] = lax.dot_general(
            chosen, omega_ref[...], (((1,), (1,)), ((), ())), preferred_element_type=F32
        ).astype(BF16)

    rows = lax.dot_general(
        lhs_ref[...], a_ref[...], (((1,), (1,)), ((), ())), preferred_element_type=F32
    )
    for i in range(4):
        refs[i][...] = rows[64 * i : 64 * i + 64]


def ordered_samples(omega, a_matrix, sent):
    depth = a_matrix.shape[1]
    block = 1024
    out = jax.ShapeDtypeStruct((64, LEAF), F32)
    return pl.pallas_call(
        functools.partial(ordered_kernel, sent=sent),
        grid=(LEAF // block,),
        in_specs=[
            pl.BlockSpec((depth, S), lambda i: (0, 0)),
            pl.BlockSpec((block, depth), lambda i: (i, 0)),
        ],
        out_specs=[pl.BlockSpec((64, block), lambda i: (0, i))] * 4,
        scratch_shapes=[pltpu.VMEM((256, depth), BF16)],
        out_shape=[out] * 4,
        compiler_params=pltpu.CompilerParams(vmem_limit_bytes=(56 if sent else 16) * 2**20),
        cost_estimate=pl.CostEstimate(
            flops=2 * 256 * depth * (LEAF + S),
            bytes_accessed=2 * depth * (LEAF + S) + 4 * 256 * LEAF,
            transcendentals=0,
        ),
        name="sent_samples" if sent else "kept_samples",
    )(omega, a_matrix)


def parts2(value):
    high = value.astype(BF16)
    return high, (value - high.astype(F32)).astype(BF16)


def product(left, right):
    return jnp.dot(left, right, preferred_element_type=F32)


def solve_kernel(*refs, packed):
    out_ref = refs[-2]
    refs[-1][...] = jnp.zeros_like(refs[-1])
    if packed:
        pieces = refs[:4]
        skeleton = jnp.concatenate([piece[:, :K] for piece in pieces], 0)
        redundant = jnp.concatenate(
            [
                piece[:, K + 32 * slot : K + 32 * slot + 32]
                for piece, slot in zip(pieces, (0, 2, 1, 3))
            ],
            0,
        )
    else:
        rest_ref, *pieces = refs[:5]
        skeleton = jnp.concatenate([piece[:, :K] for piece in pieces], 0)
        redundant = jnp.concatenate(
            [rest_ref[:, :96]] + [piece[:, K : K + 96] for piece in pieces[1:]], 0
        )
    count = redundant.shape[1]
    identity = jnp.where(
        lax.broadcasted_iota(jnp.int32, (K, K), 0) == lax.broadcasted_iota(jnp.int32, (K, K), 1),
        1.0,
        0.0,
    )

    def times(square, rows, high, low):
        rows_high, rows_low = parts2(rows)
        left = [rows_high, rows_low] if square is None else [square, rows_high, rows_low]
        first = product(jnp.concatenate(left, 0), high)
        second = product(jnp.concatenate(left[:-1], 0), low)
        start = 0 if square is None else K
        moved = (second[start:] + first[start + count :]) + first[start : start + count]
        if square is None:
            return None, moved
        mixed = second[:K]
        return first[:K] + (mixed + mixed.T), moved

    high, low = parts2(skeleton)
    gram, cross = times(parts2(skeleton.T)[0], redundant.T, high, low)
    gram = gram * (1.0 / (8.0 * S)) + identity
    bound = jnp.max(jnp.sum(jnp.abs(gram), axis=0, keepdims=True), axis=1, keepdims=True)
    power = identity - gram / bound
    out = cross / (math.sqrt(S) * bound)
    for step in range(NEWTON):
        high, low = parts2(power)
        power, moved = times(high if step < NEWTON - 1 else None, out, high, low)
        out = out + moved
    out_ref[...] = out


def solve(whole, rows, packed, after=()):
    return pl.pallas_call(
        functools.partial(solve_kernel, packed=packed),
        out_shape=[jax.ShapeDtypeStruct(shape, F32) for shape in ((rows, K), (8, 128))],
        in_specs=[VMEM] * len(whole) + [ANY] * len(after),
        out_specs=[VMEM] * 2,
        compiler_params=pltpu.CompilerParams(vmem_limit_bytes=24 * 2**20),
        cost_estimate=pl.CostEstimate(
            flops=6 * 6 * (K + rows) * K * K, bytes_accessed=4 * (S + rows) * K, transcendentals=0
        ),
        name="solve_upper" if packed else "solve_leaf",
    )(*whole, *after)


def add_kernel(kept_a, got_a, kept_b, got_b, out_a, out_b, *, first):
    rows = out_a.shape[0]
    part = slice(first, first + rows)
    out_a[...] = kept_a[part] + got_a[part]
    out_b[...] = kept_b[part] + got_b[part]


def added(kept, got, first, rows, name):
    out = jax.ShapeDtypeStruct((rows, LEAF), F32)
    return pl.pallas_call(
        functools.partial(add_kernel, first=first),
        in_specs=[VMEM] * 4,
        out_specs=[VMEM] * 2,
        out_shape=[out, out],
        compiler_params=pltpu.CompilerParams(vmem_limit_bytes=16 * 2**20),
        cost_estimate=pl.CostEstimate(
            flops=2 * rows * LEAF, bytes_accessed=24 * rows * LEAF, transcendentals=0
        ),
        name=name,
    )(kept[0], got[0], kept[1], got[1])


def parts3(value):
    high = value.astype(BF16)
    rest = value - high.astype(F32)
    middle = rest.astype(BF16)
    low = (rest - middle.astype(F32)).astype(BF16)
    return jnp.concatenate([high, middle, low], 0)


def picked(parts, order):
    place = lax.broadcasted_iota(jnp.int32, (parts.shape[1], order.shape[1]), 0)
    chosen = jnp.where(place == order, 1.0, 0.0).astype(BF16)
    moved = jnp.dot(parts, chosen, preferred_element_type=F32)
    return (moved[:32] + moved[32:64]) + moved[64:]


def finish_kernel(order_ref, *refs):
    terms, (skeleton_ref, parts_ref) = refs[:4], refs[-2:]
    half = len(terms) // 2
    totals = []
    for group in (terms[:half], terms[half:]):
        total = group[0][:16]
        for term in group[1:]:
            total = total + term[:16]
        totals.append(total)
    parts = parts3(jnp.concatenate(totals, 0))
    parts_ref[...] = parts
    skeleton_ref[...] = picked(parts, order_ref[...])


def finished(order, terms_a, terms_b, after):
    terms = [*terms_a, *terms_b]
    return pl.pallas_call(
        finish_kernel,
        in_specs=[VMEM] * (1 + len(terms)) + [ANY] * len(after),
        out_specs=[VMEM] * 2,
        out_shape=[
            jax.ShapeDtypeStruct((32, K), F32),
            jax.ShapeDtypeStruct((96, LEAF), BF16),
        ],
        compiler_params=pltpu.CompilerParams(vmem_limit_bytes=16 * 2**20),
        cost_estimate=pl.CostEstimate(
            flops=2 * 96 * LEAF * K, bytes_accessed=4 * 16 * len(terms) * LEAF, transcendentals=0
        ),
        name="finish_samples",
    )(order, *terms, *after)


def call(kernel, name, inputs, shapes, after=(), flops=10**6):
    return pl.pallas_call(
        kernel,
        in_specs=[VMEM] * len(inputs) + [ANY] * len(after),
        out_specs=[VMEM] * len(shapes),
        out_shape=[jax.ShapeDtypeStruct(shape, F32) for shape in shapes],
        compiler_params=pltpu.CompilerParams(vmem_limit_bytes=16 * 2**20),
        cost_estimate=pl.CostEstimate(flops=flops, bytes_accessed=10**6, transcendentals=0),
        name=name,
    )(*inputs, *after)


def leaf_kernel(order_ref, parts_ref, skeleton_ref, payload_ref, rest_ref):
    parts = parts_ref[...]
    payload_ref[:, :K] = skeleton_ref[...]
    for i in range(4):
        part = slice(i * K, i * K + K)
        moved = picked(parts, order_ref[:, part])
        if i < 2:
            rest_ref[:, part] = moved
        else:
            payload_ref[:, (i - 1) * K : i * K] = moved


def pack(own, rest, got, payload_ref, rest_ref):
    rows, half = own.shape[0], rest.shape[1] // 2
    payload_ref[:rows, :K] = own[:, :K]
    payload_ref[rows:, :K] = got[:, :K]
    payload_ref[:rows, K:] = rest[:, half:]
    payload_ref[rows:, K:] = got[:, K + half :]
    rest_ref[:rows] = rest[:, :half]
    rest_ref[rows:] = got[:, K : K + half]


def pack_kernel(own, rest, got, *refs):
    pack(own, rest, got, *refs[-2:])


def fork_kernel(own, rest, got, *refs):
    payload_ref, ahead_ref, rest_ref = refs[-3:]
    rows = own.shape[0]
    payload_ref[:rows, :K] = own[:, :K]
    payload_ref[rows:, :K] = got[:, :K]
    payload_ref[:rows, K:] = rest[:, 256:]
    payload_ref[rows:, K:] = got[:, K + 256 :]
    ahead_ref[:rows, :K] = own[:, :K]
    ahead_ref[rows:, :K] = got[:, :K]
    ahead_ref[:rows, K:] = rest[:, 128:256]
    ahead_ref[rows:, K:] = got[:, K + 128 : K + 256]
    rest_ref[:rows] = rest[:, :128]
    rest_ref[rows:] = got[:, K : K + 128]


def onward_kernel(got, *refs):
    refs[-1][:, :K] = got[:, :K]
    refs[-1][:, K:] = got[:, K + 128 :]


def pack_all_kernel(own, rest, got, payload_ref):
    rows = own.shape[0]
    payload_ref[:rows, :K] = own[:, :K]
    payload_ref[:rows, K:] = rest[...]
    payload_ref[rows:] = got[...]


def level_1_kernel(order, own, sibling, skeleton_ref, redundant_ref):
    moved = picked(parts3(jnp.concatenate([own[...], sibling[...]], 1)), order[...])
    skeleton_ref[...] = moved[:, :K]
    redundant_ref[...] = moved[:, K:]


def level_2_kernel(order, own, sibling, leaf, skeleton_ref, redundant_ref, payload_ref):
    level_1_kernel(order, own, sibling, skeleton_ref, redundant_ref)
    payload_ref[...] = leaf[...]


def level_3_kernel(
    order, own, sibling, leaf, rest, got, which, skeleton_1, redundant_1, redundant_2,
    upper_ref, upper_rest_ref, payload_ref, rest_ref,
):
    moved = picked(parts3(jnp.concatenate([own[...], sibling[...]], 1)), order[...])
    first, second = which[0, 0] == 0, which[0, 0] == 1
    skeleton = jnp.where(first, skeleton_1[...], jnp.where(second, own[...], moved[:, :K]))
    redundant = jnp.where(first, redundant_1[...], jnp.where(second, redundant_2[...], moved[:, K:]))
    upper_ref[:, :K] = skeleton
    upper_ref[:, K:] = redundant[:, 256:]
    upper_rest_ref[...] = redundant[:, :256]
    pack(leaf, rest, got, payload_ref, rest_ref)


def local(a_matrix, omega, leaf_pivots, upper_pivots, ranks):
    z, core, y, x = (lax.axis_index(name) for name in ("z", "core", "y", "x"))
    row_index = z * 2 + core

    near = jnp.where(core == 0, 1, 3)
    far = 4 - near
    bit = [jnp.arange(16) >> i & 1 for i in (3, 2, 1, 0)]
    leaf_owners = (y ^ bit[2] * near ^ bit[3] * far) * 4 + (x ^ bit[0] * near ^ bit[1] * far)
    upper_owners = (y ^ bit[0] * near ^ bit[3] * far) * 4 + (x ^ bit[1] * near ^ bit[2] * far)
    position = jnp.arange(K)
    leaf_order = jnp.where(position < ranks[0, row_index], leaf_pivots[0, :K], -1)[None]
    leaf_rest = jnp.take(leaf_pivots[0, K:].reshape(16, 96), leaf_owners, axis=0)
    leaf_rest = jnp.pad(leaf_rest, ((0, 0), (0, 32)), constant_values=-1).reshape(1, LEAF)
    orders = []
    for level in (1, 2, 3):
        node, side = row_index >> level, row_index >> (level - 1) & 1
        pivots = upper_pivots[level - 1, node] ^ (side << 9)
        head = jnp.where(position < ranks[level, node], pivots[:K], -1)
        rest = jnp.take(pivots[K:].reshape(16, 32), upper_owners, axis=0).reshape(K)
        orders.append(jnp.concatenate([head, rest])[None])

    near_a, both_a, near_b, both_b = ordered_samples(omega, a_matrix, True)
    got_both = hop(both_a, "x", True), hop(both_b, "y", True)
    got_near = hop(near_a, "x", True), hop(near_b, "y", True)
    own_a, far_a, own_b, far_b = ordered_samples(omega, a_matrix, False)
    send = added((far_a, far_b), got_both, 0, 64, "add_sent")
    got = hop(send[0], "x", False), hop(send[1], "y", False)
    kept = added((own_a, own_b), got_near, 0, 64, "add_kept")

    for rows, first in ((32, True), (16, False)):
        send = added(kept, got, rows, rows, "add_sent")
        kept = added(kept, got, 0, rows, "add_kept")
        got = hop(send[0], "y", first), hop(send[1], "x", first)
    leaf_skeleton, parts = finished(leaf_order, (kept[0], got[0]), (kept[1], got[1]), orders)

    small = (32, K)
    sibling = swapped(leaf_skeleton, "core", 1)
    skeleton_1, redundant_1 = call(
        level_1_kernel, "level_1", (orders[0], leaf_skeleton, sibling), (small, small)
    )
    sibling = swapped(skeleton_1, "z", 1)
    leaf, rest = call(
        leaf_kernel,
        "leaf_redundant",
        (leaf_rest, parts, leaf_skeleton),
        ((32, 3 * K), (32, 2 * K)),
        flops=2 * 96 * LEAF * LEAF,
    )
    skeleton_2, redundant_2, leaf = call(
        level_2_kernel,
        "level_2",
        (orders[1], skeleton_1, sibling, leaf),
        (small, small, (32, 3 * K)),
    )
    inner = (z ^ z >> 1) & 1
    sibling = lax.ppermute(skeleton_2, "z", [(i, i ^ 3) for i in (1, 2, 5, 6)])
    got = hop(leaf, "x", True)
    which = jnp.broadcast_to(jnp.where(core == 0, 0, 1 + inner), (1, 128)).astype(jnp.int32)
    upper, upper_rest, leaf, rest = call(
        level_3_kernel,
        "level_3",
        (orders[2], skeleton_2, sibling, leaf, rest, got, which)
        + (skeleton_1, redundant_1, redundant_2),
        ((32, K + 256), (32, 256), (64, 2 * K), (64, K)),
    )
    upper_got = hop(upper, "y", True)
    got = hop(leaf, "x", False)
    upper, upper_rest = call(
        pack_kernel, "upper_2", (upper, upper_rest, upper_got), ((64, K + 128), (64, 128))
    )
    upper_got = hop(upper, "x", True)
    leaf, ahead, rest = call(
        fork_kernel,
        "leaf_3",
        (leaf, rest, got),
        ((128, K + 256), (128, K + 128), (128, 128)),
        (upper_got,),
    )
    (upper,) = call(pack_all_kernel, "upper_3", (upper, upper_rest, upper_got), ((128, K + 128),))
    upper_got, across = hop(upper, "x", False), hop(upper, "y", False)
    got, leaf_across = hop(leaf, "y", True), hop(ahead, "y", False)
    beyond = hop(upper_got, "y", False)
    (onward,) = call(onward_kernel, "leaf_4", (got,), ((128, K + 128),), (upper_got,))
    leaf_beyond = hop(onward, "y", False)
    upper_interp, _ = solve((upper, upper_got, across, beyond), 32, True)
    other = swapped(upper_interp, "core", 1)
    leaf_interp, _ = solve((rest, leaf, got, leaf_across, leaf_beyond), 96, False, (other,))

    level_1 = jnp.where(core == 0, upper_interp, other)
    chip = jnp.where(core == 0, other, upper_interp)
    beside = swapped(chip, "z", 1)
    level_2 = jnp.where(inner == 0, chip, beside)
    level_3 = jnp.where(inner == 0, beside, chip)
    return (leaf_interp[None], jnp.stack([level_1, level_2, level_3])[:, None])


def solution(mesh):
    grid = Mesh(mesh.devices.reshape(8, 2, 4, 4), ("z", "core", "y", "x"))
    row, col = ("z", "core"), ("y", "x")
    return jax.shard_map(
        local,
        mesh=grid,
        in_specs=(P(row, col), P(col, None), P(row, None), P(), P()),
        out_specs=(P(row, col, None), P(None, row, col, None)),
        check_vma=False,
    )
```

```python
import functools
import math

import jax
import jax.numpy as jnp
from jax import lax
from jax.experimental import pallas as pl
from jax.experimental.pallas import tpu as pltpu
from jax.sharding import Mesh, PartitionSpec as P

K = 512
S = 512
LEAF = 2048
NEWTON = 6
F32 = jnp.float32
VMEM = pl.BlockSpec(memory_space=pltpu.VMEM)
ANY = pl.BlockSpec(memory_space=pl.ANY)
BF16 = jnp.bfloat16


def hop(block, axis, first):
    masks = (1, 3) if first else (3, 1)
    route = []
    for core in range(2):
        for place in range(4):
            route.append((core * 4 + place, core * 4 + (place ^ masks[core])))
    return lax.ppermute(block, ("core", axis), route)


def swapped(block, axis, mask):
    count = lax.axis_size(axis)
    return lax.ppermute(block, axis, [(i, i ^ mask) for i in range(count)])


def ordered_kernel(omega_ref, a_ref, *refs, sent):
    lhs_ref = refs[4]

    @pl.when(pl.program_id(0) == 0)
    def _():
        x, y, core = (lax.axis_index(name) for name in ("x", "y", "core"))
        near = jnp.where(core == 0, 1, 3)
        far = jnp.where(core == 0, 3, 1)
        row = lax.broadcasted_iota(jnp.int32, (256, 1), 0)
        outer = (row >> 6) & 1
        if sent:
            first = jnp.where(outer == 0, near, 2)
        else:
            first = jnp.where(outer == 0, 0, far)
        inner = (row >> 4) & 3
        second = jnp.where(
            inner == 0, 0, jnp.where(inner == 1, far, jnp.where(inner == 2, near, 2))
        )
        half_a = (x ^ first) * 64 + (y ^ second) * 16
        half_b = (x ^ second) * 64 + (y ^ first) * 16 + 256
        old = jnp.where(row < 128, half_a, half_b) + (row & 15)
        place = lax.broadcasted_iota(jnp.int32, (256, S), 1)
        chosen = jnp.where(place == old, 1.0, 0.0).astype(BF16)
        lhs_ref[...] = lax.dot_general(
            chosen, omega_ref[...], (((1,), (1,)), ((), ())), preferred_element_type=F32
        ).astype(BF16)

    rows = lax.dot_general(
        lhs_ref[...], a_ref[...], (((1,), (1,)), ((), ())), preferred_element_type=F32
    )
    for i in range(4):
        refs[i][...] = rows[64 * i : 64 * i + 64]


def ordered_samples(omega, a_matrix, sent):
    depth = a_matrix.shape[1]
    block = 1024
    out = jax.ShapeDtypeStruct((64, LEAF), F32)
    return pl.pallas_call(
        functools.partial(ordered_kernel, sent=sent),
        grid=(LEAF // block,),
        in_specs=[
            pl.BlockSpec((depth, S), lambda i: (0, 0)),
            pl.BlockSpec((block, depth), lambda i: (i, 0)),
        ],
        out_specs=[pl.BlockSpec((64, block), lambda i: (0, i))] * 4,
        scratch_shapes=[pltpu.VMEM((256, depth), BF16)],
        out_shape=[out] * 4,
        compiler_params=pltpu.CompilerParams(vmem_limit_bytes=(56 if sent else 16) * 2**20),
        cost_estimate=pl.CostEstimate(
            flops=2 * 256 * depth * (LEAF + S),
            bytes_accessed=2 * depth * (LEAF + S) + 4 * 256 * LEAF,
            transcendentals=0,
        ),
        name="sent_samples" if sent else "kept_samples",
    )(omega, a_matrix)


def parts2(value):
    high = value.astype(BF16)
    return high, (value - high.astype(F32)).astype(BF16)


def product(left, right):
    return jnp.dot(left, right, preferred_element_type=F32)


def solve_kernel(*refs, packed):
    out_ref = refs[-2]
    refs[-1][...] = jnp.zeros_like(refs[-1])
    if packed:
        pieces = refs[:4]
        skeleton = jnp.concatenate([piece[:, :K] for piece in pieces], 0)
        redundant = jnp.concatenate(
            [
                piece[:, K + 32 * slot : K + 32 * slot + 32]
                for piece, slot in zip(pieces, (0, 2, 1, 3))
            ],
            0,
        )
    else:
        rest_ref, *pieces = refs[:5]
        skeleton = jnp.concatenate([piece[:, :K] for piece in pieces], 0)
        redundant = jnp.concatenate(
            [rest_ref[:, :96]] + [piece[:, K : K + 96] for piece in pieces[1:]], 0
        )
    count = redundant.shape[1]
    identity = jnp.where(
        lax.broadcasted_iota(jnp.int32, (K, K), 0) == lax.broadcasted_iota(jnp.int32, (K, K), 1),
        1.0,
        0.0,
    )

    half = K // 2

    def times(square, rows, high, low):
        rows_high, rows_low = parts2(rows)
        if square is None:
            first = product(jnp.concatenate([rows_high, rows_low], 0), high)
            return None, (product(rows_high, low) + first[count:]) + first[:count]
        first = product(jnp.concatenate([square[:half], rows_high, rows_low], 0), high)
        corner = product(square[half:], high[:, half:])
        second = product(jnp.concatenate([square, rows_high], 0), low)
        moved = (second[K:] + first[half + count :]) + first[half : half + count]
        top = first[:half]
        main = jnp.concatenate([top, jnp.concatenate([top[:, half:].T, corner], 1)], 0)
        mixed = second[:K]
        return main + (mixed + mixed.T), moved

    high, low = parts2(skeleton)
    gram, cross = times(parts2(skeleton.T)[0], redundant.T, high, low)
    gram = gram * (1.0 / (8.0 * S)) + identity
    bound = jnp.max(jnp.sum(jnp.abs(gram), axis=0, keepdims=True), axis=1, keepdims=True)
    power = identity - gram / bound
    out = cross / (math.sqrt(S) * bound)
    for step in range(NEWTON):
        high, low = parts2(power)
        power, moved = times(high if step < NEWTON - 1 else None, out, high, low)
        out = out + moved
    out_ref[...] = out


def solve(whole, rows, packed, after=()):
    return pl.pallas_call(
        functools.partial(solve_kernel, packed=packed),
        out_shape=[jax.ShapeDtypeStruct(shape, F32) for shape in ((rows, K), (8, 128))],
        in_specs=[VMEM] * len(whole) + [ANY] * len(after),
        out_specs=[VMEM] * 2,
        compiler_params=pltpu.CompilerParams(vmem_limit_bytes=24 * 2**20),
        cost_estimate=pl.CostEstimate(
            flops=6 * 6 * (K + rows) * K * K, bytes_accessed=4 * (S + rows) * K, transcendentals=0
        ),
        name="solve_upper" if packed else "solve_leaf",
    )(*whole, *after)


def add_kernel(kept_a, got_a, kept_b, got_b, out_a, out_b, *, first):
    rows = out_a.shape[0]
    part = slice(first, first + rows)
    out_a[...] = kept_a[part] + got_a[part]
    out_b[...] = kept_b[part] + got_b[part]


def added(kept, got, first, rows, name):
    out = jax.ShapeDtypeStruct((rows, LEAF), F32)
    return pl.pallas_call(
        functools.partial(add_kernel, first=first),
        in_specs=[VMEM] * 4,
        out_specs=[VMEM] * 2,
        out_shape=[out, out],
        compiler_params=pltpu.CompilerParams(vmem_limit_bytes=16 * 2**20),
        cost_estimate=pl.CostEstimate(
            flops=2 * rows * LEAF, bytes_accessed=24 * rows * LEAF, transcendentals=0
        ),
        name=name,
    )(kept[0], got[0], kept[1], got[1])


def parts3(value):
    high = value.astype(BF16)
    rest = value - high.astype(F32)
    middle = rest.astype(BF16)
    low = (rest - middle.astype(F32)).astype(BF16)
    return jnp.concatenate([high, middle, low], 0)


def picked(parts, order):
    place = lax.broadcasted_iota(jnp.int32, (parts.shape[1], order.shape[1]), 0)
    chosen = jnp.where(place == order, 1.0, 0.0).astype(BF16)
    moved = jnp.dot(parts, chosen, preferred_element_type=F32)
    return (moved[:32] + moved[32:64]) + moved[64:]


def finish_kernel(order_ref, *refs):
    terms, (skeleton_ref, parts_ref) = refs[:4], refs[-2:]
    half = len(terms) // 2
    totals = []
    for group in (terms[:half], terms[half:]):
        total = group[0][:16]
        for term in group[1:]:
            total = total + term[:16]
        totals.append(total)
    parts = parts3(jnp.concatenate(totals, 0))
    parts_ref[...] = parts
    skeleton_ref[...] = picked(parts, order_ref[...])


def finished(order, terms_a, terms_b, after):
    terms = [*terms_a, *terms_b]
    return pl.pallas_call(
        finish_kernel,
        in_specs=[VMEM] * (1 + len(terms)) + [ANY] * len(after),
        out_specs=[VMEM] * 2,
        out_shape=[
            jax.ShapeDtypeStruct((32, K), F32),
            jax.ShapeDtypeStruct((96, LEAF), BF16),
        ],
        compiler_params=pltpu.CompilerParams(vmem_limit_bytes=16 * 2**20),
        cost_estimate=pl.CostEstimate(
            flops=2 * 96 * LEAF * K, bytes_accessed=4 * 16 * len(terms) * LEAF, transcendentals=0
        ),
        name="finish_samples",
    )(order, *terms, *after)


def call(kernel, name, inputs, shapes, after=(), flops=10**6):
    return pl.pallas_call(
        kernel,
        in_specs=[VMEM] * len(inputs) + [ANY] * len(after),
        out_specs=[VMEM] * len(shapes),
        out_shape=[jax.ShapeDtypeStruct(shape, F32) for shape in shapes],
        compiler_params=pltpu.CompilerParams(vmem_limit_bytes=16 * 2**20),
        cost_estimate=pl.CostEstimate(flops=flops, bytes_accessed=10**6, transcendentals=0),
        name=name,
    )(*inputs, *after)


def leaf_kernel(order_ref, parts_ref, skeleton_ref, payload_ref, rest_ref):
    parts = parts_ref[...]
    payload_ref[:, :K] = skeleton_ref[...]
    for i in range(4):
        part = slice(i * K, i * K + K)
        moved = picked(parts, order_ref[:, part])
        if i < 2:
            rest_ref[:, part] = moved
        else:
            payload_ref[:, (i - 1) * K : i * K] = moved


def pack(own, rest, got, payload_ref, rest_ref):
    rows, half = own.shape[0], rest.shape[1] // 2
    payload_ref[:rows, :K] = own[:, :K]
    payload_ref[rows:, :K] = got[:, :K]
    payload_ref[:rows, K:] = rest[:, half:]
    payload_ref[rows:, K:] = got[:, K + half :]
    rest_ref[:rows] = rest[:, :half]
    rest_ref[rows:] = got[:, K : K + half]


def pack_kernel(own, rest, got, *refs):
    pack(own, rest, got, *refs[-2:])


def fork_kernel(own, rest, got, *refs):
    payload_ref, ahead_ref, rest_ref = refs[-3:]
    rows = own.shape[0]
    payload_ref[:rows, :K] = own[:, :K]
    payload_ref[rows:, :K] = got[:, :K]
    payload_ref[:rows, K:] = rest[:, 256:]
    payload_ref[rows:, K:] = got[:, K + 256 :]
    ahead_ref[:rows, :K] = own[:, :K]
    ahead_ref[rows:, :K] = got[:, :K]
    ahead_ref[:rows, K:] = rest[:, 128:256]
    ahead_ref[rows:, K:] = got[:, K + 128 : K + 256]
    rest_ref[:rows] = rest[:, :128]
    rest_ref[rows:] = got[:, K : K + 128]


def onward_kernel(got, *refs):
    refs[-1][:, :K] = got[:, :K]
    refs[-1][:, K:] = got[:, K + 128 :]


def pack_all_kernel(own, rest, got, payload_ref):
    rows = own.shape[0]
    payload_ref[:rows, :K] = own[:, :K]
    payload_ref[:rows, K:] = rest[...]
    payload_ref[rows:] = got[...]


def level_1_kernel(order, own, sibling, skeleton_ref, redundant_ref):
    moved = picked(parts3(jnp.concatenate([own[...], sibling[...]], 1)), order[...])
    skeleton_ref[...] = moved[:, :K]
    redundant_ref[...] = moved[:, K:]


def level_2_kernel(order, own, sibling, leaf, skeleton_ref, redundant_ref, payload_ref):
    level_1_kernel(order, own, sibling, skeleton_ref, redundant_ref)
    payload_ref[...] = leaf[...]


def level_3_kernel(
    order, own, sibling, leaf, rest, got, which, skeleton_1, redundant_1, redundant_2,
    upper_ref, upper_rest_ref, payload_ref, rest_ref,
):
    moved = picked(parts3(jnp.concatenate([own[...], sibling[...]], 1)), order[...])
    first, second = which[0, 0] == 0, which[0, 0] == 1
    skeleton = jnp.where(first, skeleton_1[...], jnp.where(second, own[...], moved[:, :K]))
    redundant = jnp.where(first, redundant_1[...], jnp.where(second, redundant_2[...], moved[:, K:]))
    upper_ref[:, :K] = skeleton
    upper_ref[:, K:] = redundant[:, 256:]
    upper_rest_ref[...] = redundant[:, :256]
    pack(leaf, rest, got, payload_ref, rest_ref)


def orders_kernel(
    ranks_ref, leaf_ref, upper_ref, head_ref, rest_ref, one_ref, two_ref, three_ref, leaf_slots, slots
):
    z, core, y, x = (lax.axis_index(name) for name in ("z", "core", "y", "x"))
    row_index = z * 2 + core
    near = jnp.where(core == 0, 1, 3)
    far = 4 - near
    position = lax.broadcasted_iota(jnp.int32, (1, K), 1)
    head_ref[...] = jnp.where(position < ranks_ref[0, row_index], leaf_ref[:, :K], -1)
    orders = (one_ref, two_ref, three_ref)
    rests = []
    for level in (1, 2, 3):
        node, side = row_index >> level, row_index >> (level - 1) & 1
        pivots = upper_ref[level - 1, pl.ds(node, 1), :] ^ (side << 9)
        head = jnp.where(position < ranks_ref[level, node], pivots[:, :K], -1)
        orders[level - 1][:, :K] = head
        rests.append(pivots[:, K:])
    rests = jnp.concatenate(rests, 0)
    leaf_slots[...] = jnp.full_like(leaf_slots, -1)
    for i in range(16):
        leaf_slots[:, i * 128 : i * 128 + 96] = leaf_ref[:, K + i * 96 : K + i * 96 + 96]
        slots[:, i * 128 : i * 128 + 32] = rests[:, i * 32 : i * 32 + 32]
    for i in range(16):
        bit = [i >> shift & 1 for shift in (3, 2, 1, 0)]
        owner = (y ^ bit[2] * near ^ bit[3] * far) * 4 + (x ^ bit[0] * near ^ bit[1] * far)
        rest_ref[:, i * 128 : i * 128 + 128] = leaf_slots[:, pl.ds(pl.multiple_of(owner * 128, 128), 128)]
        owner = (y ^ bit[0] * near ^ bit[3] * far) * 4 + (x ^ bit[1] * near ^ bit[2] * far)
        block = slots[:, pl.ds(pl.multiple_of(owner * 128, 128), 128)]
        for level in range(3):
            orders[level][:, K + i * 32 : K + i * 32 + 32] = block[level : level + 1, :32]


def pivot_orders(ranks, leaf_pivots, upper_pivots):
    shapes = (K, LEAF, 2 * K, 2 * K, 2 * K)
    return pl.pallas_call(
        orders_kernel,
        in_specs=[pl.BlockSpec(memory_space=pltpu.SMEM), VMEM, VMEM],
        out_specs=[VMEM] * 5,
        out_shape=[jax.ShapeDtypeStruct((1, size), jnp.int32) for size in shapes],
        scratch_shapes=[pltpu.VMEM((1, LEAF), jnp.int32), pltpu.VMEM((3, LEAF), jnp.int32)],
        compiler_params=pltpu.CompilerParams(vmem_limit_bytes=16 * 2**20),
        cost_estimate=pl.CostEstimate(flops=10**6, bytes_accessed=10**5, transcendentals=0),
        name="pivot_orders",
    )(ranks, leaf_pivots, upper_pivots)


def local(a_matrix, omega, leaf_pivots, upper_pivots, ranks):
    z, core, y, x = (lax.axis_index(name) for name in ("z", "core", "y", "x"))
    leaf_order, leaf_rest, *orders = pivot_orders(ranks, leaf_pivots, upper_pivots)

    near_a, both_a, near_b, both_b = ordered_samples(omega, a_matrix, True)
    got_both = hop(both_a, "x", True), hop(both_b, "y", True)
    got_near = hop(near_a, "x", True), hop(near_b, "y", True)
    own_a, far_a, own_b, far_b = ordered_samples(omega, a_matrix, False)
    send = added((far_a, far_b), got_both, 0, 64, "add_sent")
    got = hop(send[0], "x", False), hop(send[1], "y", False)
    kept = added((own_a, own_b), got_near, 0, 64, "add_kept")

    for rows, first in ((32, True), (16, False)):
        send = added(kept, got, rows, rows, "add_sent")
        kept = added(kept, got, 0, rows, "add_kept")
        got = hop(send[0], "y", first), hop(send[1], "x", first)
    leaf_skeleton, parts = finished(leaf_order, (kept[0], got[0]), (kept[1], got[1]), orders)

    small = (32, K)
    sibling = swapped(leaf_skeleton, "core", 1)
    skeleton_1, redundant_1 = call(
        level_1_kernel, "level_1", (orders[0], leaf_skeleton, sibling), (small, small)
    )
    sibling = swapped(skeleton_1, "z", 1)
    leaf, rest = call(
        leaf_kernel,
        "leaf_redundant",
        (leaf_rest, parts, leaf_skeleton),
        ((32, 3 * K), (32, 2 * K)),
        flops=2 * 96 * LEAF * LEAF,
    )
    skeleton_2, redundant_2, leaf = call(
        level_2_kernel,
        "level_2",
        (orders[1], skeleton_1, sibling, leaf),
        (small, small, (32, 3 * K)),
    )
    inner = (z ^ z >> 1) & 1
    sibling = lax.ppermute(skeleton_2, "z", [(i, i ^ 3) for i in (1, 2, 5, 6)])
    got = hop(leaf, "x", True)
    which = jnp.broadcast_to(jnp.where(core == 0, 0, 1 + inner), (1, 128)).astype(jnp.int32)
    upper, upper_rest, leaf, rest = call(
        level_3_kernel,
        "level_3",
        (orders[2], skeleton_2, sibling, leaf, rest, got, which)
        + (skeleton_1, redundant_1, redundant_2),
        ((32, K + 256), (32, 256), (64, 2 * K), (64, K)),
    )
    upper_got = hop(upper, "y", True)
    got = hop(leaf, "x", False)
    upper, upper_rest = call(
        pack_kernel, "upper_2", (upper, upper_rest, upper_got), ((64, K + 128), (64, 128))
    )
    upper_got = hop(upper, "x", True)
    leaf, ahead, rest = call(
        fork_kernel,
        "leaf_3",
        (leaf, rest, got),
        ((128, K + 256), (128, K + 128), (128, 128)),
        (upper_got,),
    )
    (upper,) = call(pack_all_kernel, "upper_3", (upper, upper_rest, upper_got), ((128, K + 128),))
    upper_got, across = hop(upper, "x", False), hop(upper, "y", False)
    got, leaf_across = hop(leaf, "y", True), hop(ahead, "y", False)
    beyond = hop(upper_got, "y", False)
    (onward,) = call(onward_kernel, "leaf_4", (got,), ((128, K + 128),), (upper_got,))
    leaf_beyond = hop(onward, "y", False)
    upper_interp, _ = solve((upper, upper_got, across, beyond), 32, True)
    other = swapped(upper_interp, "core", 1)
    leaf_interp, _ = solve((rest, leaf, got, leaf_across, leaf_beyond), 96, False, (other,))

    level_1 = jnp.where(core == 0, upper_interp, other)
    chip = jnp.where(core == 0, other, upper_interp)
    beside = swapped(chip, "z", 1)
    level_2 = jnp.where(inner == 0, chip, beside)
    level_3 = jnp.where(inner == 0, beside, chip)
    return (leaf_interp[None], jnp.stack([level_1, level_2, level_3])[:, None])


def solution(mesh):
    grid = Mesh(mesh.devices.reshape(8, 2, 4, 4), ("z", "core", "y", "x"))
    row, col = ("z", "core"), ("y", "x")
    return jax.shard_map(
        local,
        mesh=grid,
        in_specs=(P(row, col), P(col, None), P(row, None), P(), P()),
        out_specs=(P(row, col, None), P(None, row, col, None)),
        check_vma=False,
    )
```

```python
import functools
import math

import jax
import jax.numpy as jnp
from jax import lax
from jax.experimental import pallas as pl
from jax.experimental.pallas import tpu as pltpu
from jax.sharding import Mesh, PartitionSpec as P

K = 512
S = 512
LEAF = 2048
NEWTON = 6
F32 = jnp.float32
VMEM = pl.BlockSpec(memory_space=pltpu.VMEM)
ANY = pl.BlockSpec(memory_space=pl.ANY)
BF16 = jnp.bfloat16


def hop(block, axis, first):
    masks = (1, 3) if first else (3, 1)
    route = []
    for core in range(2):
        for place in range(4):
            route.append((core * 4 + place, core * 4 + (place ^ masks[core])))
    return lax.ppermute(block, ("core", axis), route)


def swapped(block, axis, mask):
    count = lax.axis_size(axis)
    return lax.ppermute(block, axis, [(i, i ^ mask) for i in range(count)])


def ordered_kernel(omega_ref, a_ref, *refs, sent):
    lhs_ref = refs[4]

    @pl.when(pl.program_id(0) == 0)
    def _():
        x, y, core = (lax.axis_index(name) for name in ("x", "y", "core"))
        near = jnp.where(core == 0, 1, 3)
        far = jnp.where(core == 0, 3, 1)
        row = lax.broadcasted_iota(jnp.int32, (256, 1), 0)
        outer = (row >> 6) & 1
        if sent:
            first = jnp.where(outer == 0, near, 2)
        else:
            first = jnp.where(outer == 0, 0, far)
        inner = (row >> 4) & 3
        second = jnp.where(
            inner == 0, 0, jnp.where(inner == 1, far, jnp.where(inner == 2, near, 2))
        )
        half_a = (x ^ first) * 64 + (y ^ second) * 16
        half_b = (x ^ second) * 64 + (y ^ first) * 16 + 256
        old = jnp.where(row < 128, half_a, half_b) + (row & 15)
        place = lax.broadcasted_iota(jnp.int32, (256, S), 1)
        chosen = jnp.where(place == old, 1.0, 0.0).astype(BF16)
        lhs_ref[...] = lax.dot_general(
            chosen, omega_ref[...], (((1,), (1,)), ((), ())), preferred_element_type=F32
        ).astype(BF16)

    rows = lax.dot_general(
        lhs_ref[...], a_ref[...], (((1,), (1,)), ((), ())), preferred_element_type=F32
    )
    for i in range(4):
        refs[i][...] = rows[64 * i : 64 * i + 64]


def ordered_samples(omega, a_matrix, sent):
    depth = a_matrix.shape[1]
    block = 1024
    out = jax.ShapeDtypeStruct((64, LEAF), F32)
    return pl.pallas_call(
        functools.partial(ordered_kernel, sent=sent),
        grid=(LEAF // block,),
        in_specs=[
            pl.BlockSpec((depth, S), lambda i: (0, 0)),
            pl.BlockSpec((block, depth), lambda i: (i, 0)),
        ],
        out_specs=[pl.BlockSpec((64, block), lambda i: (0, i))] * 4,
        scratch_shapes=[pltpu.VMEM((256, depth), BF16)],
        out_shape=[out] * 4,
        compiler_params=pltpu.CompilerParams(vmem_limit_bytes=(56 if sent else 16) * 2**20),
        cost_estimate=pl.CostEstimate(
            flops=2 * 256 * depth * (LEAF + S),
            bytes_accessed=2 * depth * (LEAF + S) + 4 * 256 * LEAF,
            transcendentals=0,
        ),
        name="sent_samples" if sent else "kept_samples",
    )(omega, a_matrix)


def parts2(value):
    high = value.astype(BF16)
    return high, (value - high.astype(F32)).astype(BF16)


def product(left, right):
    return jnp.dot(left, right, preferred_element_type=F32)


def solve_kernel(*refs, packed):
    out_ref = refs[-2]
    refs[-1][...] = jnp.zeros_like(refs[-1])
    if packed:
        pieces = refs[:4]
        skeleton = jnp.concatenate([piece[:, :K] for piece in pieces], 0)
        redundant = jnp.concatenate(
            [
                piece[:, K + 32 * slot : K + 32 * slot + 32]
                for piece, slot in zip(pieces, (0, 2, 1, 3))
            ],
            0,
        )
    else:
        rest_ref, *pieces = refs[:5]
        skeleton = jnp.concatenate([piece[:, :K] for piece in pieces], 0)
        redundant = jnp.concatenate(
            [rest_ref[:, :96]] + [piece[:, K : K + 96] for piece in pieces[1:]], 0
        )
    count = redundant.shape[1]
    identity = jnp.where(
        lax.broadcasted_iota(jnp.int32, (K, K), 0) == lax.broadcasted_iota(jnp.int32, (K, K), 1),
        1.0,
        0.0,
    )

    half = K // 2

    def times(square, rows, high, low):
        rows_high, rows_low = parts2(rows)
        if square is None:
            first = product(jnp.concatenate([rows_high, rows_low], 0), high)
            return None, (product(rows_high, low) + first[count:]) + first[:count]
        first = product(jnp.concatenate([square[:half], rows_high, rows_low], 0), high)
        corner = product(square[half:], high[:, half:])
        second = product(jnp.concatenate([square, rows_high], 0), low)
        moved = (second[K:] + first[half + count :]) + first[half : half + count]
        top = first[:half]
        main = jnp.concatenate([top, jnp.concatenate([top[:, half:].T, corner], 1)], 0)
        mixed = second[:K]
        return main + (mixed + mixed.T), moved

    high, low = parts2(skeleton)
    gram, cross = times(parts2(skeleton.T)[0], redundant.T, high, low)
    gram = gram * (1.0 / (8.0 * S)) + identity
    bound = jnp.max(jnp.sum(jnp.abs(gram), axis=0, keepdims=True), axis=1, keepdims=True)
    power = identity - gram / bound
    out = cross / (math.sqrt(S) * bound)
    for step in range(NEWTON):
        high, low = parts2(power)
        power, moved = times(high if step < NEWTON - 1 else None, out, high, low)
        out = out + moved
    out_ref[...] = out


def solve(whole, rows, packed, after=()):
    return pl.pallas_call(
        functools.partial(solve_kernel, packed=packed),
        out_shape=[jax.ShapeDtypeStruct(shape, F32) for shape in ((rows, K), (8, 128))],
        in_specs=[VMEM] * len(whole) + [ANY] * len(after),
        out_specs=[VMEM] * 2,
        compiler_params=pltpu.CompilerParams(vmem_limit_bytes=24 * 2**20),
        cost_estimate=pl.CostEstimate(
            flops=6 * 6 * (K + rows) * K * K, bytes_accessed=4 * (S + rows) * K, transcendentals=0
        ),
        name="solve_upper" if packed else "solve_leaf",
    )(*whole, *after)


def add_kernel(kept_a, got_a, kept_b, got_b, out_a, out_b, *, first):
    rows = out_a.shape[0]
    part = slice(first, first + rows)
    out_a[...] = kept_a[part] + got_a[part]
    out_b[...] = kept_b[part] + got_b[part]


def added(kept, got, first, rows, name):
    out = jax.ShapeDtypeStruct((rows, LEAF), F32)
    return pl.pallas_call(
        functools.partial(add_kernel, first=first),
        in_specs=[VMEM] * 4,
        out_specs=[VMEM] * 2,
        out_shape=[out, out],
        compiler_params=pltpu.CompilerParams(vmem_limit_bytes=16 * 2**20),
        cost_estimate=pl.CostEstimate(
            flops=2 * rows * LEAF, bytes_accessed=24 * rows * LEAF, transcendentals=0
        ),
        name=name,
    )(kept[0], got[0], kept[1], got[1])


def parts3(value):
    high = value.astype(BF16)
    rest = value - high.astype(F32)
    middle = rest.astype(BF16)
    low = (rest - middle.astype(F32)).astype(BF16)
    return jnp.concatenate([high, middle, low], 0)


def picked(parts, order):
    place = lax.broadcasted_iota(jnp.int32, (parts.shape[1], order.shape[1]), 0)
    chosen = jnp.where(place == order, 1.0, 0.0).astype(BF16)
    moved = jnp.dot(parts, chosen, preferred_element_type=F32)
    return (moved[:32] + moved[32:64]) + moved[64:]


def finish_kernel(order_ref, *refs):
    terms, (skeleton_ref, parts_ref) = refs[:4], refs[-2:]
    half = len(terms) // 2
    totals = []
    for group in (terms[:half], terms[half:]):
        total = group[0][:16]
        for term in group[1:]:
            total = total + term[:16]
        totals.append(total)
    parts = parts3(jnp.concatenate(totals, 0))
    parts_ref[...] = parts
    skeleton_ref[...] = picked(parts, order_ref[...])


def finished(order, terms_a, terms_b, after):
    terms = [*terms_a, *terms_b]
    return pl.pallas_call(
        finish_kernel,
        in_specs=[VMEM] * (1 + len(terms)) + [ANY] * len(after),
        out_specs=[VMEM] * 2,
        out_shape=[
            jax.ShapeDtypeStruct((32, K), F32),
            jax.ShapeDtypeStruct((96, LEAF), BF16),
        ],
        compiler_params=pltpu.CompilerParams(vmem_limit_bytes=16 * 2**20),
        cost_estimate=pl.CostEstimate(
            flops=2 * 96 * LEAF * K, bytes_accessed=4 * 16 * len(terms) * LEAF, transcendentals=0
        ),
        name="finish_samples",
    )(order, *terms, *after)


def call(kernel, name, inputs, shapes, after=(), flops=10**6):
    return pl.pallas_call(
        kernel,
        in_specs=[VMEM] * len(inputs) + [ANY] * len(after),
        out_specs=[VMEM] * len(shapes),
        out_shape=[jax.ShapeDtypeStruct(shape, F32) for shape in shapes],
        compiler_params=pltpu.CompilerParams(vmem_limit_bytes=16 * 2**20),
        cost_estimate=pl.CostEstimate(flops=flops, bytes_accessed=10**6, transcendentals=0),
        name=name,
    )(*inputs, *after)


def leaf_kernel(order_ref, parts_ref, skeleton_ref, payload_ref, rest_ref):
    parts = parts_ref[...]
    payload_ref[:, :K] = skeleton_ref[...]
    for i in range(4):
        part = slice(i * K, i * K + K)
        moved = picked(parts, order_ref[:, part])
        if i < 2:
            rest_ref[:, part] = moved
        else:
            payload_ref[:, (i - 1) * K : i * K] = moved


def pack(own, rest, got, payload_ref, rest_ref):
    rows, half = own.shape[0], rest.shape[1] // 2
    payload_ref[:rows, :K] = own[:, :K]
    payload_ref[rows:, :K] = got[:, :K]
    payload_ref[:rows, K:] = rest[:, half:]
    payload_ref[rows:, K:] = got[:, K + half :]
    rest_ref[:rows] = rest[:, :half]
    rest_ref[rows:] = got[:, K : K + half]


def pack_kernel(own, rest, got, *refs):
    pack(own, rest, got, *refs[-2:])


def fork_kernel(own, rest, got, *refs):
    payload_ref, ahead_ref, rest_ref = refs[-3:]
    rows = own.shape[0]
    payload_ref[:rows, :K] = own[:, :K]
    payload_ref[rows:, :K] = got[:, :K]
    payload_ref[:rows, K:] = rest[:, 256:]
    payload_ref[rows:, K:] = got[:, K + 256 :]
    ahead_ref[:rows, :K] = own[:, :K]
    ahead_ref[rows:, :K] = got[:, :K]
    ahead_ref[:rows, K:] = rest[:, 128:256]
    ahead_ref[rows:, K:] = got[:, K + 128 : K + 256]
    rest_ref[:rows] = rest[:, :128]
    rest_ref[rows:] = got[:, K : K + 128]


def onward_kernel(got, *refs):
    refs[-1][:, :K] = got[:, :K]
    refs[-1][:, K:] = got[:, K + 128 :]


def pack_all_kernel(own, rest, got, payload_ref):
    rows = own.shape[0]
    payload_ref[:rows, :K] = own[:, :K]
    payload_ref[:rows, K:] = rest[...]
    payload_ref[rows:] = got[...]


def level_1_kernel(order, own, sibling, skeleton_ref, redundant_ref):
    moved = picked(parts3(jnp.concatenate([own[...], sibling[...]], 1)), order[...])
    skeleton_ref[...] = moved[:, :K]
    redundant_ref[...] = moved[:, K:]


def level_2_kernel(order, own, sibling, leaf, skeleton_ref, redundant_ref, payload_ref):
    level_1_kernel(order, own, sibling, skeleton_ref, redundant_ref)
    payload_ref[...] = leaf[...]


def level_3_kernel(
    order, own, sibling, leaf, rest, got, which, skeleton_1, redundant_1, redundant_2,
    upper_ref, upper_rest_ref, payload_ref, rest_ref,
):
    moved = picked(parts3(jnp.concatenate([own[...], sibling[...]], 1)), order[...])
    first, second = which[0, 0] == 0, which[0, 0] == 1
    skeleton = jnp.where(first, skeleton_1[...], jnp.where(second, own[...], moved[:, :K]))
    redundant = jnp.where(first, redundant_1[...], jnp.where(second, redundant_2[...], moved[:, K:]))
    upper_ref[:, :K] = skeleton
    upper_ref[:, K:] = redundant[:, 256:]
    upper_rest_ref[...] = redundant[:, :256]
    pack(leaf, rest, got, payload_ref, rest_ref)


def orders_kernel(
    ranks_ref, leaf_ref, upper_ref, head_ref, rest_ref, one_ref, two_ref, three_ref, leaf_slots, slots
):
    z, core, y, x = (lax.axis_index(name) for name in ("z", "core", "y", "x"))
    row_index = z * 2 + core
    near = jnp.where(core == 0, 1, 3)
    far = 4 - near
    position = lax.broadcasted_iota(jnp.int32, (1, K), 1)
    head_ref[...] = jnp.where(position < ranks_ref[0, row_index], leaf_ref[:, :K], -1)
    orders = (one_ref, two_ref, three_ref)
    rests = []
    for level in (1, 2, 3):
        node, side = row_index >> level, row_index >> (level - 1) & 1
        pivots = upper_ref[level - 1, pl.ds(node, 1), :] ^ (side << 9)
        head = jnp.where(position < ranks_ref[level, node], pivots[:, :K], -1)
        orders[level - 1][:, :K] = head
        rests.append(pivots[:, K:])
    rests = jnp.concatenate(rests, 0)
    leaf_slots[...] = jnp.full_like(leaf_slots, -1)
    for i in range(16):
        leaf_slots[:, i * 128 : i * 128 + 96] = leaf_ref[:, K + i * 96 : K + i * 96 + 96]
        slots[:, i * 128 : i * 128 + 32] = rests[:, i * 32 : i * 32 + 32]
    for i in range(16):
        bit = [i >> shift & 1 for shift in (3, 2, 1, 0)]
        owner = (y ^ bit[2] * near ^ bit[3] * far) * 4 + (x ^ bit[0] * near ^ bit[1] * far)
        rest_ref[:, i * 128 : i * 128 + 128] = leaf_slots[:, pl.ds(pl.multiple_of(owner * 128, 128), 128)]
        owner = (y ^ bit[0] * near ^ bit[3] * far) * 4 + (x ^ bit[1] * near ^ bit[2] * far)
        block = slots[:, pl.ds(pl.multiple_of(owner * 128, 128), 128)]
        for level in range(3):
            orders[level][:, K + i * 32 : K + i * 32 + 32] = block[level : level + 1, :32]


def pivot_orders(ranks, leaf_pivots, upper_pivots):
    shapes = (K, LEAF, 2 * K, 2 * K, 2 * K)
    return pl.pallas_call(
        orders_kernel,
        in_specs=[pl.BlockSpec(memory_space=pltpu.SMEM), VMEM, VMEM],
        out_specs=[VMEM] * 5,
        out_shape=[jax.ShapeDtypeStruct((1, size), jnp.int32) for size in shapes],
        scratch_shapes=[pltpu.VMEM((1, LEAF), jnp.int32), pltpu.VMEM((3, LEAF), jnp.int32)],
        compiler_params=pltpu.CompilerParams(vmem_limit_bytes=16 * 2**20),
        cost_estimate=pl.CostEstimate(flops=10**6, bytes_accessed=10**5, transcendentals=0),
        name="pivot_orders",
    )(ranks, leaf_pivots, upper_pivots)


def local(a_matrix, omega, leaf_pivots, upper_pivots, ranks):
    z, core, y, x = (lax.axis_index(name) for name in ("z", "core", "y", "x"))
    leaf_order, leaf_rest, *orders = pivot_orders(ranks, leaf_pivots, upper_pivots)

    near_a, both_a, near_b, both_b = ordered_samples(omega, a_matrix, True)
    got_both = hop(both_a, "x", True), hop(both_b, "y", True)
    got_near = hop(near_a, "x", True), hop(near_b, "y", True)
    own_a, far_a, own_b, far_b = ordered_samples(omega, a_matrix, False)
    send = added((far_a, far_b), got_both, 32, 32, "add_sent")
    got_ahead = hop(send[0], "x", False), hop(send[1], "y", False)
    send = added((far_a, far_b), got_both, 0, 32, "add_sent")
    got = hop(send[0], "x", False), hop(send[1], "y", False)
    send = added((own_a, own_b), got_near, 32, 32, "add_kept")
    kept = added((own_a, own_b), got_near, 0, 32, "add_kept")
    send = added(send, got_ahead, 0, 32, "add_sent")
    kept = added(kept, got, 0, 32, "add_kept")
    got = hop(send[0], "y", True), hop(send[1], "x", True)
    send = added(kept, got, 16, 16, "add_sent")
    kept = added(kept, got, 0, 16, "add_kept")
    got = hop(send[0], "y", False), hop(send[1], "x", False)
    leaf_skeleton, parts = finished(leaf_order, (kept[0], got[0]), (kept[1], got[1]), orders)

    small = (32, K)
    sibling = swapped(leaf_skeleton, "core", 1)
    skeleton_1, redundant_1 = call(
        level_1_kernel, "level_1", (orders[0], leaf_skeleton, sibling), (small, small)
    )
    sibling = swapped(skeleton_1, "z", 1)
    leaf, rest = call(
        leaf_kernel,
        "leaf_redundant",
        (leaf_rest, parts, leaf_skeleton),
        ((32, 3 * K), (32, 2 * K)),
        flops=2 * 96 * LEAF * LEAF,
    )
    skeleton_2, redundant_2, leaf = call(
        level_2_kernel,
        "level_2",
        (orders[1], skeleton_1, sibling, leaf),
        (small, small, (32, 3 * K)),
    )
    inner = (z ^ z >> 1) & 1
    sibling = lax.ppermute(skeleton_2, "z", [(i, i ^ 3) for i in (1, 2, 5, 6)])
    got = hop(leaf, "x", True)
    which = jnp.broadcast_to(jnp.where(core == 0, 0, 1 + inner), (1, 128)).astype(jnp.int32)
    upper, upper_rest, leaf, rest = call(
        level_3_kernel,
        "level_3",
        (orders[2], skeleton_2, sibling, leaf, rest, got, which)
        + (skeleton_1, redundant_1, redundant_2),
        ((32, K + 256), (32, 256), (64, 2 * K), (64, K)),
    )
    upper_got = hop(upper, "y", True)
    got = hop(leaf, "x", False)
    upper, upper_rest = call(
        pack_kernel, "upper_2", (upper, upper_rest, upper_got), ((64, K + 128), (64, 128))
    )
    upper_got = hop(upper, "x", True)
    leaf, ahead, rest = call(
        fork_kernel,
        "leaf_3",
        (leaf, rest, got),
        ((128, K + 256), (128, K + 128), (128, 128)),
        (upper_got,),
    )
    (upper,) = call(pack_all_kernel, "upper_3", (upper, upper_rest, upper_got), ((128, K + 128),))
    upper_got, across = hop(upper, "x", False), hop(upper, "y", False)
    got, leaf_across = hop(leaf, "y", True), hop(ahead, "y", False)
    beyond = hop(upper_got, "y", False)
    (onward,) = call(onward_kernel, "leaf_4", (got,), ((128, K + 128),), (upper_got,))
    leaf_beyond = hop(onward, "y", False)
    upper_interp, _ = solve((upper, upper_got, across, beyond), 32, True)
    other = swapped(upper_interp, "core", 1)
    leaf_interp, _ = solve((rest, leaf, got, leaf_across, leaf_beyond), 96, False, (other,))

    level_1 = jnp.where(core == 0, upper_interp, other)
    chip = jnp.where(core == 0, other, upper_interp)
    beside = swapped(chip, "z", 1)
    level_2 = jnp.where(inner == 0, chip, beside)
    level_3 = jnp.where(inner == 0, beside, chip)
    return (leaf_interp[None], jnp.stack([level_1, level_2, level_3])[:, None])


def solution(mesh):
    grid = Mesh(mesh.devices.reshape(8, 2, 4, 4), ("z", "core", "y", "x"))
    row, col = ("z", "core"), ("y", "x")
    return jax.shard_map(
        local,
        mesh=grid,
        in_specs=(P(row, col), P(col, None), P(row, None), P(), P()),
        out_specs=(P(row, col, None), P(None, row, col, None)),
        check_vma=False,
    )
```

```python
import functools
import math

import jax
import jax.numpy as jnp
from jax import lax
from jax.experimental import pallas as pl
from jax.experimental.pallas import tpu as pltpu
from jax.sharding import Mesh, PartitionSpec as P

K = 512
S = 512
LEAF = 2048
NEWTON = 6
F32 = jnp.float32
VMEM = pl.BlockSpec(memory_space=pltpu.VMEM)
ANY = pl.BlockSpec(memory_space=pl.ANY)
BF16 = jnp.bfloat16


def hop(block, axis, first):
    masks = (1, 3) if first else (3, 1)
    route = []
    for core in range(2):
        for place in range(4):
            route.append((core * 4 + place, core * 4 + (place ^ masks[core])))
    return lax.ppermute(block, ("core", axis), route)


def swapped(block, axis, mask):
    count = lax.axis_size(axis)
    return lax.ppermute(block, axis, [(i, i ^ mask) for i in range(count)])


def ordered_kernel(omega_ref, a_ref, *refs, sent):
    outs, lhs_ref = refs[:-1], refs[-1]

    @pl.when(pl.program_id(0) == 0)
    def _():
        x, y, core = (lax.axis_index(name) for name in ("x", "y", "core"))
        near = jnp.where(core == 0, 1, 3)
        far = jnp.where(core == 0, 3, 1)
        row = lax.broadcasted_iota(jnp.int32, (256, 1), 0)
        outer = (row >> 6) & 1
        if sent:
            first = jnp.where(outer == 0, near, 2)
        else:
            first = jnp.where(outer == 0, 0, far)
        inner = (row >> 4) & 3
        second = jnp.where(
            inner == 0, 0, jnp.where(inner == 1, far, jnp.where(inner == 2, near, 2))
        )
        half_a = (x ^ first) * 64 + (y ^ second) * 16
        half_b = (x ^ second) * 64 + (y ^ first) * 16 + 256
        old = jnp.where(row < 128, half_a, half_b) + (row & 15)
        place = lax.broadcasted_iota(jnp.int32, (256, S), 1)
        chosen = jnp.where(place == old, 1.0, 0.0).astype(BF16)
        lhs_ref[...] = lax.dot_general(
            chosen, omega_ref[...], (((1,), (1,)), ((), ())), preferred_element_type=F32
        ).astype(BF16)

    rows = lax.dot_general(
        lhs_ref[...], a_ref[...], (((1,), (1,)), ((), ())), preferred_element_type=F32
    )
    low = 0
    for out_ref in outs:
        size = out_ref.shape[0]
        out_ref[...] = rows[low : low + size]
        low += size


def ordered_samples(omega, a_matrix, sent):
    sizes = (64, 32, 32) * 2 if sent else (64, 64) * 2
    depth = a_matrix.shape[1]
    block = 1024
    return pl.pallas_call(
        functools.partial(ordered_kernel, sent=sent),
        grid=(LEAF // block,),
        in_specs=[
            pl.BlockSpec((depth, S), lambda i: (0, 0)),
            pl.BlockSpec((block, depth), lambda i: (i, 0)),
        ],
        out_specs=[pl.BlockSpec((size, block), lambda i: (0, i)) for size in sizes],
        scratch_shapes=[pltpu.VMEM((256, depth), BF16)],
        out_shape=[jax.ShapeDtypeStruct((size, LEAF), F32) for size in sizes],
        compiler_params=pltpu.CompilerParams(vmem_limit_bytes=(56 if sent else 16) * 2**20),
        cost_estimate=pl.CostEstimate(
            flops=2 * 256 * depth * (LEAF + S),
            bytes_accessed=2 * depth * (LEAF + S) + 4 * 256 * LEAF,
            transcendentals=0,
        ),
        name="sent_samples" if sent else "kept_samples",
    )(omega, a_matrix)


def parts2(value):
    high = value.astype(BF16)
    return high, (value - high.astype(F32)).astype(BF16)


def product(left, right):
    return jnp.dot(left, right, preferred_element_type=F32)


def solve_kernel(*refs, packed):
    out_ref = refs[-2]
    refs[-1][...] = jnp.zeros_like(refs[-1])
    if packed:
        pieces = refs[:4]
        skeleton = jnp.concatenate([piece[:, :K] for piece in pieces], 0)
        redundant = jnp.concatenate(
            [
                piece[:, K + 32 * slot : K + 32 * slot + 32]
                for piece, slot in zip(pieces, (0, 2, 1, 3))
            ],
            0,
        )
    else:
        rest_ref, *pieces = refs[:5]
        skeleton = jnp.concatenate([piece[:, :K] for piece in pieces], 0)
        redundant = jnp.concatenate(
            [rest_ref[:, :96]] + [piece[:, K : K + 96] for piece in pieces[1:]], 0
        )
    count = redundant.shape[1]
    identity = jnp.where(
        lax.broadcasted_iota(jnp.int32, (K, K), 0) == lax.broadcasted_iota(jnp.int32, (K, K), 1),
        1.0,
        0.0,
    )

    half = K // 2

    def times(square, rows, high, low):
        rows_high, rows_low = parts2(rows)
        if square is None:
            first = product(jnp.concatenate([rows_high, rows_low], 0), high)
            return None, (product(rows_high, low) + first[count:]) + first[:count]
        first = product(jnp.concatenate([square[:half], rows_high, rows_low], 0), high)
        corner = product(square[half:], high[:, half:])
        second = product(jnp.concatenate([square, rows_high], 0), low)
        moved = (second[K:] + first[half + count :]) + first[half : half + count]
        top = first[:half]
        main = jnp.concatenate([top, jnp.concatenate([top[:, half:].T, corner], 1)], 0)
        mixed = second[:K]
        return main + (mixed + mixed.T), moved

    high, low = parts2(skeleton)
    gram, cross = times(parts2(skeleton.T)[0], redundant.T, high, low)
    gram = gram * (1.0 / (8.0 * S)) + identity
    bound = jnp.max(jnp.sum(jnp.abs(gram), axis=0, keepdims=True), axis=1, keepdims=True)
    power = identity - gram / bound
    out = cross / (math.sqrt(S) * bound)
    for step in range(NEWTON):
        high, low = parts2(power)
        power, moved = times(high if step < NEWTON - 1 else None, out, high, low)
        out = out + moved
    out_ref[...] = out


def solve(whole, rows, packed, after=()):
    return pl.pallas_call(
        functools.partial(solve_kernel, packed=packed),
        out_shape=[jax.ShapeDtypeStruct(shape, F32) for shape in ((rows, K), (8, 128))],
        in_specs=[VMEM] * len(whole) + [ANY] * len(after),
        out_specs=[VMEM] * 2,
        compiler_params=pltpu.CompilerParams(vmem_limit_bytes=24 * 2**20),
        cost_estimate=pl.CostEstimate(
            flops=6 * 6 * (K + rows) * K * K, bytes_accessed=4 * (S + rows) * K, transcendentals=0
        ),
        name="solve_upper" if packed else "solve_leaf",
    )(*whole, *after)


def add_kernel(kept_a, got_a, kept_b, got_b, out_a, out_b, *, first):
    rows = out_a.shape[0]
    part = slice(first, first + rows)
    got_part = part if got_a.shape[0] > rows else slice(0, rows)
    out_a[...] = kept_a[part] + got_a[got_part]
    out_b[...] = kept_b[part] + got_b[got_part]


def added(kept, got, first, rows, name):
    out = jax.ShapeDtypeStruct((rows, LEAF), F32)
    return pl.pallas_call(
        functools.partial(add_kernel, first=first),
        in_specs=[VMEM] * 4,
        out_specs=[VMEM] * 2,
        out_shape=[out, out],
        compiler_params=pltpu.CompilerParams(vmem_limit_bytes=16 * 2**20),
        cost_estimate=pl.CostEstimate(
            flops=2 * rows * LEAF, bytes_accessed=24 * rows * LEAF, transcendentals=0
        ),
        name=name,
    )(kept[0], got[0], kept[1], got[1])


def parts3(value):
    high = value.astype(BF16)
    rest = value - high.astype(F32)
    middle = rest.astype(BF16)
    low = (rest - middle.astype(F32)).astype(BF16)
    return jnp.concatenate([high, middle, low], 0)


def picked(parts, order):
    place = lax.broadcasted_iota(jnp.int32, (parts.shape[1], order.shape[1]), 0)
    chosen = jnp.where(place == order, 1.0, 0.0).astype(BF16)
    moved = jnp.dot(parts, chosen, preferred_element_type=F32)
    return (moved[:32] + moved[32:64]) + moved[64:]


def finish_kernel(order_ref, *refs):
    terms, (skeleton_ref, parts_ref) = refs[:4], refs[-2:]
    half = len(terms) // 2
    totals = []
    for group in (terms[:half], terms[half:]):
        total = group[0][:16]
        for term in group[1:]:
            total = total + term[:16]
        totals.append(total)
    parts = parts3(jnp.concatenate(totals, 0))
    parts_ref[...] = parts
    skeleton_ref[...] = picked(parts, order_ref[...])


def finished(order, terms_a, terms_b, after):
    terms = [*terms_a, *terms_b]
    return pl.pallas_call(
        finish_kernel,
        in_specs=[VMEM] * (1 + len(terms)) + [ANY] * len(after),
        out_specs=[VMEM] * 2,
        out_shape=[
            jax.ShapeDtypeStruct((32, K), F32),
            jax.ShapeDtypeStruct((96, LEAF), BF16),
        ],
        compiler_params=pltpu.CompilerParams(vmem_limit_bytes=16 * 2**20),
        cost_estimate=pl.CostEstimate(
            flops=2 * 96 * LEAF * K, bytes_accessed=4 * 16 * len(terms) * LEAF, transcendentals=0
        ),
        name="finish_samples",
    )(order, *terms, *after)


def call(kernel, name, inputs, shapes, after=(), flops=10**6):
    return pl.pallas_call(
        kernel,
        in_specs=[VMEM] * len(inputs) + [ANY] * len(after),
        out_specs=[VMEM] * len(shapes),
        out_shape=[jax.ShapeDtypeStruct(shape, F32) for shape in shapes],
        compiler_params=pltpu.CompilerParams(vmem_limit_bytes=16 * 2**20),
        cost_estimate=pl.CostEstimate(flops=flops, bytes_accessed=10**6, transcendentals=0),
        name=name,
    )(*inputs, *after)


def leaf_kernel(order_ref, parts_ref, skeleton_ref, payload_ref, rest_ref):
    parts = parts_ref[...]
    payload_ref[:, :K] = skeleton_ref[...]
    for i in range(4):
        part = slice(i * K, i * K + K)
        moved = picked(parts, order_ref[:, part])
        if i < 2:
            rest_ref[:, part] = moved
        else:
            payload_ref[:, (i - 1) * K : i * K] = moved


def pack(own, rest, got, payload_ref, rest_ref):
    rows, half = own.shape[0], rest.shape[1] // 2
    payload_ref[:rows, :K] = own[:, :K]
    payload_ref[rows:, :K] = got[:, :K]
    payload_ref[:rows, K:] = rest[:, half:]
    payload_ref[rows:, K:] = got[:, K + half :]
    rest_ref[:rows] = rest[:, :half]
    rest_ref[rows:] = got[:, K : K + half]


def pack_kernel(own, rest, got, *refs):
    pack(own, rest, got, *refs[-2:])


def fork_kernel(own, rest, got, *refs):
    payload_ref, ahead_ref, rest_ref = refs[-3:]
    rows = own.shape[0]
    payload_ref[:rows, :K] = own[:, :K]
    payload_ref[rows:, :K] = got[:, :K]
    payload_ref[:rows, K:] = rest[:, 256:]
    payload_ref[rows:, K:] = got[:, K + 256 :]
    ahead_ref[:rows, :K] = own[:, :K]
    ahead_ref[rows:, :K] = got[:, :K]
    ahead_ref[:rows, K:] = rest[:, 128:256]
    ahead_ref[rows:, K:] = got[:, K + 128 : K + 256]
    rest_ref[:rows] = rest[:, :128]
    rest_ref[rows:] = got[:, K : K + 128]


def onward_kernel(got, *refs):
    refs[-1][:, :K] = got[:, :K]
    refs[-1][:, K:] = got[:, K + 128 :]


def pack_all_kernel(own, rest, got, payload_ref):
    rows = own.shape[0]
    payload_ref[:rows, :K] = own[:, :K]
    payload_ref[:rows, K:] = rest[...]
    payload_ref[rows:] = got[...]


def level_1_kernel(order, own, sibling, skeleton_ref, redundant_ref):
    moved = picked(parts3(jnp.concatenate([own[...], sibling[...]], 1)), order[...])
    skeleton_ref[...] = moved[:, :K]
    redundant_ref[...] = moved[:, K:]


def level_2_kernel(order, own, sibling, leaf, skeleton_ref, redundant_ref, payload_ref):
    level_1_kernel(order, own, sibling, skeleton_ref, redundant_ref)
    payload_ref[...] = leaf[...]


def level_3_kernel(
    order, own, sibling, leaf, rest, got, which, skeleton_1, redundant_1, redundant_2,
    upper_ref, upper_rest_ref, payload_ref, rest_ref,
):
    moved = picked(parts3(jnp.concatenate([own[...], sibling[...]], 1)), order[...])
    first, second = which[0, 0] == 0, which[0, 0] == 1
    skeleton = jnp.where(first, skeleton_1[...], jnp.where(second, own[...], moved[:, :K]))
    redundant = jnp.where(first, redundant_1[...], jnp.where(second, redundant_2[...], moved[:, K:]))
    upper_ref[:, :K] = skeleton
    upper_ref[:, K:] = redundant[:, 256:]
    upper_rest_ref[...] = redundant[:, :256]
    pack(leaf, rest, got, payload_ref, rest_ref)


def orders_kernel(
    ranks_ref, leaf_ref, upper_ref, head_ref, rest_ref, one_ref, two_ref, three_ref, leaf_slots, slots
):
    z, core, y, x = (lax.axis_index(name) for name in ("z", "core", "y", "x"))
    row_index = z * 2 + core
    near = jnp.where(core == 0, 1, 3)
    far = 4 - near
    position = lax.broadcasted_iota(jnp.int32, (1, K), 1)
    head_ref[...] = jnp.where(position < ranks_ref[0, row_index], leaf_ref[:, :K], -1)
    orders = (one_ref, two_ref, three_ref)
    rests = []
    for level in (1, 2, 3):
        node, side = row_index >> level, row_index >> (level - 1) & 1
        pivots = upper_ref[level - 1, pl.ds(node, 1), :] ^ (side << 9)
        head = jnp.where(position < ranks_ref[level, node], pivots[:, :K], -1)
        orders[level - 1][:, :K] = head
        rests.append(pivots[:, K:])
    rests = jnp.concatenate(rests, 0)
    leaf_slots[...] = jnp.full_like(leaf_slots, -1)
    for i in range(16):
        leaf_slots[:, i * 128 : i * 128 + 96] = leaf_ref[:, K + i * 96 : K + i * 96 + 96]
        slots[:, i * 128 : i * 128 + 32] = rests[:, i * 32 : i * 32 + 32]
    for i in range(16):
        bit = [i >> shift & 1 for shift in (3, 2, 1, 0)]
        owner = (y ^ bit[2] * near ^ bit[3] * far) * 4 + (x ^ bit[0] * near ^ bit[1] * far)
        rest_ref[:, i * 128 : i * 128 + 128] = leaf_slots[:, pl.ds(pl.multiple_of(owner * 128, 128), 128)]
        owner = (y ^ bit[0] * near ^ bit[3] * far) * 4 + (x ^ bit[1] * near ^ bit[2] * far)
        block = slots[:, pl.ds(pl.multiple_of(owner * 128, 128), 128)]
        for level in range(3):
            orders[level][:, K + i * 32 : K + i * 32 + 32] = block[level : level + 1, :32]


def pivot_orders(ranks, leaf_pivots, upper_pivots):
    shapes = (K, LEAF, 2 * K, 2 * K, 2 * K)
    return pl.pallas_call(
        orders_kernel,
        in_specs=[pl.BlockSpec(memory_space=pltpu.SMEM), VMEM, VMEM],
        out_specs=[VMEM] * 5,
        out_shape=[jax.ShapeDtypeStruct((1, size), jnp.int32) for size in shapes],
        scratch_shapes=[pltpu.VMEM((1, LEAF), jnp.int32), pltpu.VMEM((3, LEAF), jnp.int32)],
        compiler_params=pltpu.CompilerParams(vmem_limit_bytes=16 * 2**20),
        cost_estimate=pl.CostEstimate(flops=10**6, bytes_accessed=10**5, transcendentals=0),
        name="pivot_orders",
    )(ranks, leaf_pivots, upper_pivots)


def local(a_matrix, omega, leaf_pivots, upper_pivots, ranks):
    z, core, y, x = (lax.axis_index(name) for name in ("z", "core", "y", "x"))
    leaf_order, leaf_rest, *orders = pivot_orders(ranks, leaf_pivots, upper_pivots)

    near_a, low_a, high_a, near_b, low_b, high_b = ordered_samples(omega, a_matrix, True)
    got_high = hop(high_a, "x", True), hop(high_b, "y", True)
    got_low = hop(low_a, "x", True), hop(low_b, "y", True)
    got_near = hop(near_a, "x", True), hop(near_b, "y", True)
    own_a, far_a, own_b, far_b = ordered_samples(omega, a_matrix, False)
    send = added((far_a, far_b), got_high, 32, 32, "add_sent")
    got_ahead = hop(send[0], "x", False), hop(send[1], "y", False)
    send = added((far_a, far_b), got_low, 0, 32, "add_sent")
    got = hop(send[0], "x", False), hop(send[1], "y", False)
    send = added((own_a, own_b), got_near, 32, 32, "add_kept")
    kept = added((own_a, own_b), got_near, 0, 32, "add_kept")
    send = added(send, got_ahead, 0, 32, "add_sent")
    kept = added(kept, got, 0, 32, "add_kept")
    got = hop(send[0], "y", True), hop(send[1], "x", True)
    send = added(kept, got, 16, 16, "add_sent")
    kept = added(kept, got, 0, 16, "add_kept")
    got = hop(send[0], "y", False), hop(send[1], "x", False)
    leaf_skeleton, parts = finished(leaf_order, (kept[0], got[0]), (kept[1], got[1]), orders)

    small = (32, K)
    sibling = swapped(leaf_skeleton, "core", 1)
    skeleton_1, redundant_1 = call(
        level_1_kernel, "level_1", (orders[0], leaf_skeleton, sibling), (small, small)
    )
    sibling = swapped(skeleton_1, "z", 1)
    leaf, rest = call(
        leaf_kernel,
        "leaf_redundant",
        (leaf_rest, parts, leaf_skeleton),
        ((32, 3 * K), (32, 2 * K)),
        flops=2 * 96 * LEAF * LEAF,
    )
    skeleton_2, redundant_2, leaf = call(
        level_2_kernel,
        "level_2",
        (orders[1], skeleton_1, sibling, leaf),
        (small, small, (32, 3 * K)),
    )
    inner = (z ^ z >> 1) & 1
    sibling = lax.ppermute(skeleton_2, "z", [(i, i ^ 3) for i in (1, 2, 5, 6)])
    got = hop(leaf, "x", True)
    which = jnp.broadcast_to(jnp.where(core == 0, 0, 1 + inner), (1, 128)).astype(jnp.int32)
    upper, upper_rest, leaf, rest = call(
        level_3_kernel,
        "level_3",
        (orders[2], skeleton_2, sibling, leaf, rest, got, which)
        + (skeleton_1, redundant_1, redundant_2),
        ((32, K + 256), (32, 256), (64, 2 * K), (64, K)),
    )
    upper_got = hop(upper, "y", True)
    got = hop(leaf, "x", False)
    upper, upper_rest = call(
        pack_kernel, "upper_2", (upper, upper_rest, upper_got), ((64, K + 128), (64, 128))
    )
    upper_got = hop(upper, "x", True)
    leaf, ahead, rest = call(
        fork_kernel,
        "leaf_3",
        (leaf, rest, got),
        ((128, K + 256), (128, K + 128), (128, 128)),
        (upper_got,),
    )
    (upper,) = call(pack_all_kernel, "upper_3", (upper, upper_rest, upper_got), ((128, K + 128),))
    upper_got, across = hop(upper, "x", False), hop(upper, "y", False)
    got, leaf_across = hop(leaf, "y", True), hop(ahead, "y", False)
    beyond = hop(upper_got, "y", False)
    (onward,) = call(onward_kernel, "leaf_4", (got,), ((128, K + 128),), (upper_got,))
    leaf_beyond = hop(onward, "y", False)
    upper_interp, _ = solve((upper, upper_got, across, beyond), 32, True)
    other = swapped(upper_interp, "core", 1)
    leaf_interp, _ = solve((rest, leaf, got, leaf_across, leaf_beyond), 96, False, (other,))

    level_1 = jnp.where(core == 0, upper_interp, other)
    chip = jnp.where(core == 0, other, upper_interp)
    beside = swapped(chip, "z", 1)
    level_2 = jnp.where(inner == 0, chip, beside)
    level_3 = jnp.where(inner == 0, beside, chip)
    return (leaf_interp[None], jnp.stack([level_1, level_2, level_3])[:, None])


def solution(mesh):
    grid = Mesh(mesh.devices.reshape(8, 2, 4, 4), ("z", "core", "y", "x"))
    row, col = ("z", "core"), ("y", "x")
    return jax.shard_map(
        local,
        mesh=grid,
        in_specs=(P(row, col), P(col, None), P(row, None), P(), P()),
        out_specs=(P(row, col, None), P(None, row, col, None)),
        check_vma=False,
    )
```
